128 devices in a mesh: row: 4 (over x_hi, core), col: 4 (over z), depth: 8 (over y, x_lo).
Axes of the slice: x: 4 (x_hi: 2, x_lo: 2; x = x_hi * 2 + x_lo), y: 4, z: 4, core: 2. Of those that a mesh axis runs over, the one named last changes fastest.
Arguments:
- a_blocks: bfloat16 [32, 4, 4, 16, 128, 128], P(None, 'col', 'row', 'depth'), may hold values from -6 to 6
- a_rows: int32 [32, 4, 4, 16], replicated, may hold values from -1 to 31, as said below
- b_blocks: bfloat16 [32, 4, 4, 8, 128, 128], P(None, 'row', 'col', 'depth'), may hold values from -0.15625 to 0.15625
- b_cols: int32 [32, 4, 4, 8], replicated, may hold values from -1 to 15, as said below
- c_pos: int32 [4, 4, 128], P('row', 'col'), may hold values from -1 to 511, as said below
Outputs:
- c_blocks: bfloat16 [4, 4, 128, 128, 128], P('row', 'col', 'depth')
The draws below stay inside these ranges and needn't reach their ends.
Inputs may be any that keep to these rules, and one draw needn't show every extreme that they name: `a_rows`: for each inner block (g, m) and row group i the live slots come first and hold distinct local block rows, the rest hold -1; each has at least one live slot, and in every draw some (g, m, i) has all 16 slots live. `b_cols`: for each inner block (g, m) and column group h the live slots come first and hold distinct local block columns, the rest hold -1; each has at least one live slot, and in every draw some (g, m, h) has all 8 slots live. `c_pos`: each cell lists distinct positions in its first slots and -1 in the rest; every cell keeps at least one block, and in every draw some cell keeps 128.
All inputs are finite; a program needn't handle non-finite values.
Results may differ from the reference program's by a relative error of at most 0.001.
Values may be sent and summed in bfloat16 or wider, within the bound.
A program may use at most 320 MiB of HBM per device.

```python
import jax
import jax.numpy as jnp
from jax import lax

BS = 128
MBL = 32
NBL = 16
KPD = 4
SA = 16
SB = 8
NCL = 128
RG = 4
CG = 4
KG = 32


def slot_rows(key, count, slots, span):
    order_key, live_key, full_key = jax.random.split(key, 3)
    order_keys = jax.random.split(order_key, count)
    orders = jax.vmap(lambda one_key: jax.random.permutation(one_key, span))(order_keys)[:, :slots].astype(jnp.int32)
    live_count = jax.random.randint(live_key, (count, 1), 1, slots + 1)
    chosen = jax.random.randint(full_key, (), 0, count)
    live_count = jnp.where(jnp.arange(count)[:, None] == chosen, slots, live_count)
    position = jnp.arange(slots)[None, :]
    return jnp.where(position < live_count, orders, -1).astype(jnp.int32)


def draw_a_rows(key, part):
    key = jax.random.fold_in(key, 11)
    return slot_rows(key, KG * KPD * RG, SA, MBL).reshape(KG, KPD, RG, SA)


def draw_b_cols(key, part):
    key = jax.random.fold_in(key, 23)
    return slot_rows(key, KG * KPD * CG, SB, NBL).reshape(KG, KPD, CG, SB)


def draw_c_pos(key, part):
    key = jax.random.fold_in(key, 37)
    return slot_rows(key, RG * CG, NCL, MBL * NBL).reshape(RG, CG, NCL)


def block_scale(key, shape, cuts, smallest, top_value):
    level, own = 1.0, jax.random.fold_in(key, 6)
    for axis_at, blocks in cuts:
        heights = jnp.exp(jax.random.uniform(jax.random.fold_in(own, axis_at), (blocks,), jnp.float32, smallest / len(cuts), top_value / len(cuts)))
        level = level * jnp.repeat(heights, shape[axis_at] // blocks).reshape([-1 if axis == axis_at else 1 for axis in range(len(shape))])
    return level


def scatter_about(key, shape, spread, bound, pieces=(), held_as=jnp.bfloat16):
    entries = spread * jax.random.normal(key, shape, jnp.float32)
    if pieces:
        entries = entries * block_scale(key, shape, pieces, -0.22, 0.18)
    return jnp.clip(entries, -bound, bound).astype(held_as)


def setup_inputs(seed: int = 0) -> dict:
    streams_of = jax.random.split(jax.random.key(seed), 6)
    a_blocks = scatter_about(streams_of[0], (KG, KPD, RG, SA, BS, BS), 1.0, 6.0, ((1, 4), (2, 4), (3, 8)))
    a_rows = draw_a_rows(jax.random.fold_in(streams_of[5], 71), 0)
    b_blocks = scatter_about(streams_of[2], (KG, KPD, CG, SB, BS, BS), (BS * KG * KPD * (SA + 1) * (SB + 1) // (4 * MBL * NBL)) ** -0.5, 0.15625, ((1, 4), (2, 4), (3, 8)))
    b_cols = draw_b_cols(jax.random.fold_in(streams_of[5], 71), 0)
    c_pos = draw_c_pos(jax.random.fold_in(streams_of[5], 71), 0)
    return {"a_blocks": a_blocks, "a_rows": a_rows, "b_blocks": b_blocks, "b_cols": b_cols, "c_pos": c_pos}


def reference(a_blocks, a_rows, b_blocks, b_cols, c_pos):
    block_side = a_blocks.shape[-1]
    cell_area = MBL * NBL
    slot_count = RG * CG * NCL
    labels = jnp.arange(slot_count, dtype=jnp.int32).reshape(RG, CG, NCL)
    cell_row = jnp.arange(RG, dtype=jnp.int32)[:, None, None] + jnp.zeros((RG, CG, NCL), jnp.int32)
    cell_col = jnp.arange(CG, dtype=jnp.int32)[None, :, None] + jnp.zeros((RG, CG, NCL), jnp.int32)
    spot_index = jnp.where(c_pos >= 0, c_pos, cell_area).astype(jnp.int32)
    slot_table = jnp.full((RG, CG, cell_area), slot_count, jnp.int32)
    slot_table = slot_table.at[cell_row, cell_col, spot_index].set(labels, mode="drop")
    inner_count = KG * KPD
    a_flat = a_blocks.reshape(inner_count, RG, SA, block_side, block_side)
    r_flat = a_rows.reshape(inner_count, RG, SA)
    b_flat = b_blocks.reshape(inner_count, CG, SB, block_side, block_side)
    c_flat = b_cols.reshape(inner_count, CG, SB)
    rows_idx = jnp.arange(RG, dtype=jnp.int32)[:, None, None, None]
    cols_idx = jnp.arange(CG, dtype=jnp.int32)[None, :, None, None]

    def add_inner(running_sum, inner_parts):
        a_one, r_one, b_one, c_one = inner_parts
        products = jnp.einsum("iuxy,hvyz->ihuvxz", a_one.astype(jnp.float32), b_one.astype(jnp.float32), precision=lax.Precision.HIGHEST)
        usable = (r_one[:, None, :, None] >= 0) & (c_one[None, :, None, :] >= 0)
        spot_here = r_one[:, None, :, None] * NBL + c_one[None, :, None, :]
        spot_here = jnp.where(usable, spot_here, 0).astype(jnp.int32)
        target = slot_table[rows_idx, cols_idx, spot_here]
        target = jnp.where(usable, target, slot_count).astype(jnp.int32)
        running_sum = running_sum.at[target.reshape(-1)].add(products.reshape(-1, block_side, block_side), mode="drop")
        return running_sum, None

    running_sum = jnp.zeros((slot_count, block_side, block_side), jnp.float32)
    running_sum, _ = lax.scan(add_inner, running_sum, (a_flat, r_flat, b_flat, c_flat))
    return running_sum.reshape(RG, CG, NCL, block_side, block_side).astype(jnp.bfloat16)
```

```python
import functools

import jax
import jax.numpy as jnp
from jax import lax
from jax.experimental import pallas as pl
from jax.experimental.pallas import tpu as pltpu
from jax.sharding import PartitionSpec as P

MESH = pl.DeviceIdType.MESH
BS = 128
NBL = 16
MBL = 32
ANY = pl.BlockSpec(memory_space=pl.ANY)
SMEM = pl.BlockSpec(memory_space=pltpu.SMEM)


def place():
    row, z, depth = lax.axis_index("row"), lax.axis_index("col"), lax.axis_index("depth")
    return row // 2, depth % 2, row % 2, depth // 2, z


def device(x_hi, x_lo, core, y, z):
    return (x_hi * 2 + core, z, y * 2 + x_lo)


def remote(src, dst, send, recv, to):
    return pltpu.make_async_remote_copy(
        src_ref=src, dst_ref=dst, send_sem=send, recv_sem=recv, device_id=to, device_id_type=MESH
    )


PIECES = ((0, 0), (0, 1), (1, 0), (1, 1), (3, 0), (3, 1), (2, 0), (2, 1))
LAG = 2


def gather_kernel(
    a_ref, b_ref, c_ref, pa_ref, pb_ref, cs_ref, a_send, a_recv, az_send, b_send, b_recv, bx_send, c_sem
):
    x_hi, x_lo, core, y, z = place()
    x = x_hi * 2 + x_lo
    same = x_lo == core

    def y_at(step):
        return lax.rem(y + step + 4, 4)

    def z_to(step):
        return device(x_hi, x_lo, core, y, lax.rem(z + step + 4, 4))

    def x_to(step):
        to = lax.rem(x + step + 4, 4)
        return device(to // 2, lax.rem(to, 2), core, y, z)

    twin = device(x_hi, x_lo, 1 - core, y, z)

    barrier = pltpu.get_barrier_semaphore()

    def greet(to):
        pl.semaphore_signal(barrier, inc=1, device_id=to, device_id_type=MESH)

    for dy in range(4):
        for other in range(2):
            if (dy, other) == (0, 0):

                @pl.when(jnp.logical_not(same))
                def _():
                    greet(device(x_hi, x_lo, x_lo, y, z))

            else:
                lo = x_lo if other == 0 else 1 - x_lo
                greet(device(x_hi, lo, x_lo, y_at(-dy), z))
            if (dy, other) != (0, 0):
                greet(device(x_hi, x_lo, core if other == 0 else 1 - core, y_at(-dy), z))
    for step in (1, -1):
        greet(z_to(step))
        greet(x_to(step))
    apart = jnp.where(same, 0, 1)
    pl.semaphore_wait(barrier, 18 + apart)

    d_here = y * 2 + x_lo
    m_here = x_hi * 2 + core
    a_out, b_out = [], []
    for j, (dy, other) in enumerate(PIECES):
        to_y = y_at(dy)
        to_core = core if other == 0 else 1 - core
        layer = to_y * 2 + to_core
        src = a_ref.at[pl.ds(layer * 4, 4)]
        dst = pa_ref.at[z, d_here]
        sem = a_recv.at[0, dy * 2 + apart]
        copy = remote(src, dst, a_send.at[j], sem, device(x_hi, core, to_core, to_y, z))
        if (dy, other) == (0, 0):
            stay = pltpu.make_async_copy(src, dst, sem)

            @pl.when(same)
            def _():
                stay.start()

            @pl.when(jnp.logical_not(same))
            def _():
                copy.start()

            first_out = copy
        else:
            copy.start()
            a_out.append(copy)
    copy = remote(c_ref, cs_ref, c_sem.at[0], c_sem.at[1], twin)
    copy.start()
    c_out = copy
    for j, (dy, other) in enumerate(PIECES):
        to_y = y_at(dy)
        to_core = core if other == 0 else 1 - core
        layer = to_y * 2 + to_core
        src = b_ref.at[pl.ds(layer * 4, 4)]
        dst = pb_ref.at[m_here, d_here]
        sem = b_recv.at[0, dy * 2 + other]
        if (dy, other) == (0, 0):
            pltpu.make_async_copy(src, dst, sem).start()
        else:
            copy = remote(src, dst, b_send.at[j], sem, device(x_hi, x_lo, to_core, to_y, z))
            copy.start()
            b_out.append(copy)

    def a_slot(back, dy, other):
        lo = x_lo if other == 0 else 1 - x_lo
        return pa_ref.at[lax.rem(z - back + 4, 4), y_at(-dy) * 2 + lo]

    def b_slot(back, dy, other):
        from_x = lax.rem(x - back + 4, 4)
        from_core = core if other == 0 else 1 - core
        return pb_ref.at[(from_x // 2) * 2 + from_core, y_at(-dy) * 2 + lax.rem(from_x, 2)]

    def turn(slot, recv, send, to, out, j):
        dy, other = PIECES[j]
        n = dy * 2 + other
        here = slot(0, dy, other)
        remote(here, here, send.at[0, n], recv.at[0, n], to(1)).wait_recv()
        for way, step in ((0, 1), (1, -1)):
            copy = remote(here, here, send.at[way, n], recv.at[1 if step == 1 else 3, n], to(step))
            copy.start()
            out.append(copy)

    def pass_on(slot, recv, send, to, out, j):
        dy, other = PIECES[j]
        n = dy * 2 + other
        back, step = (1, 1) if j % 2 == 0 else (3, -1)
        piece = slot(back, dy, other)
        remote(piece, piece, send.at[2, n], recv.at[back, n], to(step)).wait_recv()
        copy = remote(piece, piece, send.at[2, n], recv.at[2, n], to(step))
        copy.start()
        out.append(copy)

    a_args = (a_slot, a_recv, az_send, z_to, a_out)
    b_args = (b_slot, b_recv, bx_send, x_to, b_out)
    for j in range(8 + LAG):
        if j < 8:
            turn(*a_args, j)
            turn(*b_args, j)
        if j >= LAG:
            pass_on(*a_args, j - LAG)
            pass_on(*b_args, j - LAG)
    for j, (dy, other) in enumerate(PIECES):
        n = dy * 2 + other
        for back in (3 if j % 2 == 0 else 1, 2):
            piece = a_slot(back, dy, other)
            remote(piece, piece, az_send.at[0, n], a_recv.at[back, n], z_to(1)).wait_recv()
            piece = b_slot(back, dy, other)
            remote(piece, piece, bx_send.at[0, n], b_recv.at[back, n], x_to(1)).wait_recv()
    for copy in a_out + b_out:
        copy.wait_send()
    c_out.wait()

    @pl.when(jnp.logical_not(same))
    def _():
        first_out.wait_send()


def gather_panels(a_local, b_local, c_pos):
    dma = pltpu.SemaphoreType.DMA
    return pl.pallas_call(
        gather_kernel,
        out_shape=(
            jax.ShapeDtypeStruct((4, 8, 4, 2, BS, BS), jnp.bfloat16),
            jax.ShapeDtypeStruct((4, 8, 4, BS, BS), jnp.bfloat16),
            jax.ShapeDtypeStruct(c_pos.shape, jnp.int32),
        ),
        in_specs=[ANY] * 3,
        out_specs=(ANY,) * 3,
        scratch_shapes=[
            dma((8,)), dma((4, 8)), dma((3, 8)), dma((8,)), dma((4, 8)), dma((3, 8)), dma((2,)),
        ],
        compiler_params=pltpu.CompilerParams(collective_id=0, has_side_effects=True),
        name="gather_panels",
    )(a_local, b_local, c_pos)


BATCH = 4
TABLE = (MBL + 1) * (NBL + 1) + 15


def product_kernel(
    rows_ref, cols_ref, mine_ref, twin_ref, pa_ref, pb_ref, out_ref, a_buf, b_buf, total, table, jobs, sem
):
    _, x_lo, core, _, _ = place()
    loads = [
        pltpu.make_async_copy(pa_ref, a_buf, sem.at[0]),
        pltpu.make_async_copy(pb_ref, b_buf, sem.at[1]),
    ]
    for load in loads:
        load.start()

    def clear(at, _):
        table[at] = -1
        return 0

    lax.fori_loop(0, TABLE, clear, 0, unroll=16)

    def enter(slot, _):
        spot = jnp.where(x_lo == core, mine_ref[0, 0, slot], twin_ref[0, 0, slot])
        at = (spot // NBL + 1) * (NBL + 1) + spot % NBL + 1
        table[jnp.where(spot >= 0, at, 0)] = jnp.where(spot >= 0, slot, -1)
        return 0

    lax.fori_loop(0, BS, enter, 0, unroll=8)

    def inner(k, count):
        g, m = k // 4, k % 4
        cols = [cols_ref[k, v] + 1 for v in range(8)]

        def one_row(u, count):
            at = (rows_ref[k, u] + 1) * (NBL + 1)
            a_at = ((m * 8 + u // 2) * 4 + g) * 2 + u % 2
            for v in range(8):
                slot = table[at + cols[v]]
                jobs[count] = (a_at * 128 + ((m * 8 + v) * 4 + g)) * 256 + slot
                count = count + jnp.where(slot >= 0, 1, 0)
            return count

        return lax.fori_loop(0, rows_ref[k, 16], one_row, count)

    count = lax.fori_loop(0, 16, inner, 0)
    for extra in range(BATCH):
        jobs[count + extra] = BS

    def blank(slot, _):
        total[slot] = jnp.zeros((BS, BS), jnp.float32)
        return 0

    lax.fori_loop(0, BS + 1, blank, 0)
    for load in loads:
        load.wait()

    def batch(at, _):
        slots, terms = [], []
        for n in range(BATCH):
            job = jobs[at * BATCH + n]
            slots.append(job % 256)
            terms.append(
                jnp.dot(
                    a_buf[job // 32768], b_buf[(job // 256) % 128], preferred_element_type=jnp.float32
                )
            )
        for slot, term in zip(slots, terms):
            total[slot] += term
        return 0

    lax.fori_loop(0, (count + BATCH - 1) // BATCH, batch, 0)
    store = pltpu.make_async_copy(total.at[pl.ds(0, BS)], out_ref, sem.at[0])
    store.start()
    store.wait()


def partial_sums(rows, cols, mine, twin, panel_a, panel_b):
    return pl.pallas_call(
        product_kernel,
        out_shape=jax.ShapeDtypeStruct((BS, BS, BS), jnp.float32),
        in_specs=[SMEM] * 4 + [ANY] * 2,
        out_specs=ANY,
        scratch_shapes=[
            pltpu.VMEM(panel_a.shape, jnp.bfloat16),
            pltpu.VMEM(panel_b.shape, jnp.bfloat16),
            pltpu.VMEM((BS + 1, BS, BS), jnp.float32),
            pltpu.SMEM((TABLE,), jnp.int32),
            pltpu.SMEM((16 * 128 + BATCH,), jnp.int32),
            pltpu.SemaphoreType.DMA((2,)),
        ],
        compiler_params=pltpu.CompilerParams(vmem_limit_bytes=40 * 2**20),
        name="partial_sums",
    )(rows, cols, mine, twin, panel_a, panel_b)


def reduce_kernel(
    part_ref, out_ref, own, other, via, got, done, load_sem, twin_sem, via_sem, got_sem, out_sem
):
    x_hi, x_lo, core, y, z = place()
    same = x_lo == core

    def y_at(step):
        return lax.rem(y + step + 4, 4)

    def y_to(step):
        return device(x_hi, x_lo, core, y_at(step), z)

    twin = device(x_hi, x_lo, 1 - core, y, z)
    owner = device(x_hi, core, x_lo, y, z)

    barrier = pltpu.get_barrier_semaphore()

    def greet(to):
        pl.semaphore_signal(barrier, inc=1, device_id=to, device_id_type=MESH)

    greet(twin)
    greet(y_to(1))
    greet(y_to(-1))

    @pl.when(jnp.logical_not(same))
    def _():
        greet(owner)

    pl.semaphore_wait(barrier, 3 + jnp.where(same, 0, 1))

    order = (2, 1, 3, 0)
    loads, twins, sent = {}, {}, []
    for r in order:
        loads[r] = pltpu.make_async_copy(part_ref.at[y_at(r), core], own.at[r], load_sem.at[r])
        loads[r].start()
        twins[r] = remote(
            part_ref.at[y_at(r), 1 - core], other.at[r], twin_sem.at[0, r], twin_sem.at[1, r], twin
        )
        twins[r].start()

    def add(into, r, first, count, term):
        def one(n, _):
            into[r, first + n] += term[n]
            return 0

        lax.fori_loop(0, count, one, 0)

    def meet(r):
        loads[r].wait()
        twins[r].wait_recv()
        add(own, r, 0, 16, other.at[r])

    def send(src, dst, sems, to):
        copy = remote(src, dst, sems[0], sems[1], to)
        copy.start()
        sent.append(copy)
        return copy

    def pair(sems, n):
        return sems.at[0, n], sems.at[1, n]

    meet(2)
    via_up = send(own.at[2, pl.ds(0, 8)], via.at[0], pair(via_sem, 0), y_to(1))
    via_down = send(own.at[2, pl.ds(8, 8)], via.at[1], pair(via_sem, 1), y_to(-1))
    meet(1)
    up_late = send(own.at[1, pl.ds(8, 8)], got.at[0, pl.ds(8, 8)], pair(got_sem, 0), y_to(1))
    meet(3)
    down_early = send(own.at[3, pl.ds(0, 8)], got.at[1, pl.ds(0, 8)], pair(got_sem, 1), y_to(-1))
    via_up.wait_recv()
    add(own, 1, 0, 8, via.at[0])
    up_early = send(own.at[1, pl.ds(0, 8)], got.at[0, pl.ds(0, 8)], pair(got_sem, 2), y_to(1))
    via_down.wait_recv()
    add(own, 3, 8, 8, via.at[1])
    down_late = send(own.at[3, pl.ds(8, 8)], got.at[1, pl.ds(8, 8)], pair(got_sem, 3), y_to(-1))
    meet(0)
    up_late.wait_recv()
    add(own, 0, 8, 8, got.at[0, pl.ds(8, 8)])
    down_early.wait_recv()
    add(own, 0, 0, 8, got.at[1, pl.ds(0, 8)])

    def finish(half, from_way):
        first = half * 8

        def one(n, _):
            done[first + n] = (own[0, first + n] + got[from_way, first + n]).astype(jnp.bfloat16)
            return 0

        lax.fori_loop(0, 8, one, 0)
        span = pl.ds(first, 8)

        @pl.when(same)
        def _():
            pltpu.make_async_copy(done.at[span], out_ref.at[span], out_sem.at[1, half]).start()

        @pl.when(jnp.logical_not(same))
        def _():
            remote(done.at[span], out_ref.at[span], out_sem.at[0, half], out_sem.at[1, half], owner).start()

    up_early.wait_recv()
    finish(0, 0)
    down_late.wait_recv()
    finish(1, 1)
    for half in range(2):
        span = pl.ds(half * 8, 8)
        copy = remote(done.at[span], out_ref.at[span], out_sem.at[0, half], out_sem.at[1, half], owner)
        copy.wait_recv()

        @pl.when(jnp.logical_not(same))
        def _():
            copy.wait_send()

    for copy in sent:
        copy.wait_send()
    for r in order:
        twins[r].wait_send()


def reduce_sums(part):
    dma = pltpu.SemaphoreType.DMA
    f32 = jnp.float32
    return pl.pallas_call(
        reduce_kernel,
        out_shape=jax.ShapeDtypeStruct((16, BS, BS), jnp.bfloat16),
        in_specs=[ANY],
        out_specs=ANY,
        scratch_shapes=[
            pltpu.VMEM((4, 16, BS, BS), f32),
            pltpu.VMEM((4, 16, BS, BS), f32),
            pltpu.VMEM((2, 8, BS, BS), f32),
            pltpu.VMEM((2, 16, BS, BS), f32),
            pltpu.VMEM((16, BS, BS), jnp.bfloat16),
            dma((4,)), dma((2, 4)), dma((2, 2)), dma((2, 4)), dma((2, 2)),
        ],
        compiler_params=pltpu.CompilerParams(
            collective_id=1, has_side_effects=True, vmem_limit_bytes=40 * 2**20
        ),
        name="reduce_sums",
    )(part)


def per_device(a_blocks, a_rows, b_blocks, b_cols, c_pos):
    x_hi, x_lo, core, y, z = place()
    layer = y * 2 + core
    rows = lax.dynamic_slice(a_rows, (layer * 4, 0, x_hi * 2 + x_lo, 0), (4, 4, 1, 16)).reshape(16, 16)
    rows = jnp.concatenate([rows, jnp.sum(rows >= 0, axis=1, keepdims=True, dtype=jnp.int32)], axis=1)
    cols = lax.dynamic_slice(b_cols, (layer * 4, 0, z, 0), (4, 4, 1, 8)).reshape(16, 8)
    panel_a, panel_b, twin_pos = gather_panels(a_blocks[:, 0, 0], b_blocks[:, 0, 0, 0], c_pos)
    part = partial_sums(
        rows, cols, c_pos, twin_pos, panel_a.reshape(256, BS, BS), panel_b.reshape(128, BS, BS)
    )
    return reduce_sums(part.reshape(4, 2, 16, BS, BS))[None, None]


def solution(mesh):
    placed = (
        P(None, "col", "row", "depth", None, None),
        P(),
        P(None, "row", "col", "depth", None, None),
        P(),
        P("row", "col", None),
    )
    return jax.shard_map(
        per_device,
        mesh=mesh,
        in_specs=placed,
        out_specs=P("row", "col", "depth", None, None),
        check_vma=False,
    )
```

```python
import functools

import jax
import jax.numpy as jnp
from jax import lax
from jax.experimental import pallas as pl
from jax.experimental.pallas import tpu as pltpu
from jax.sharding import PartitionSpec as P

MESH = pl.DeviceIdType.MESH
BS = 128
NBL = 16
ANY = pl.BlockSpec(memory_space=pl.ANY)


def place():
    row, z, depth = lax.axis_index("row"), lax.axis_index("col"), lax.axis_index("depth")
    return row // 2, depth % 2, row % 2, depth // 2, z


def device(x_hi, x_lo, core, y, z):
    return (x_hi * 2 + core, z, y * 2 + x_lo)


def remote(src, dst, send, recv, to):
    return pltpu.make_async_remote_copy(
        src_ref=src, dst_ref=dst, send_sem=send, recv_sem=recv, device_id=to, device_id_type=MESH
    )


PIECES = ((0, 0), (0, 1), (1, 0), (1, 1), (3, 0), (3, 1), (2, 0), (2, 1))
SCHEDULE = (
    "ta0", "tb0", "ta1", "tb1", "ta2", "pa0", "ta3", "pa1", "ta4", "pa2", "ta5", "pa3", "ta6",
    "pa4", "ta7", "tb2", "pb0", "tb3", "pb1", "tb4", "pb2", "tb5", "pb3", "pa5", "tb6", "pb4",
    "tb7", "pa6", "pb5", "pa7", "pb6", "pb7",
)


def gather_kernel(
    a_ref, b_ref, c_ref, pa_ref, pb_ref, cs_ref, a_send, a_recv, az_send, b_send, b_recv, bx_send, c_sem
):
    x_hi, x_lo, core, y, z = place()
    x = x_hi * 2 + x_lo
    same = x_lo == core

    def y_at(step):
        return lax.rem(y + step + 4, 4)

    def z_to(step):
        return device(x_hi, x_lo, core, y, lax.rem(z + step + 4, 4))

    def x_to(step):
        to = lax.rem(x + step + 4, 4)
        return device(to // 2, lax.rem(to, 2), core, y, z)

    twin = device(x_hi, x_lo, 1 - core, y, z)

    barrier = pltpu.get_barrier_semaphore()

    def greet(to):
        pl.semaphore_signal(barrier, inc=1, device_id=to, device_id_type=MESH)

    for dy in range(4):
        for other in range(2):
            if (dy, other) == (0, 0):

                @pl.when(jnp.logical_not(same))
                def _():
                    greet(device(x_hi, x_lo, x_lo, y, z))

            else:
                lo = x_lo if other == 0 else 1 - x_lo
                greet(device(x_hi, lo, x_lo, y_at(-dy), z))
            if (dy, other) != (0, 0):
                greet(device(x_hi, x_lo, core if other == 0 else 1 - core, y_at(-dy), z))
    for step in (1, -1):
        greet(z_to(step))
        greet(x_to(step))
    apart = jnp.where(same, 0, 1)
    pl.semaphore_wait(barrier, 18 + apart)

    d_here = y * 2 + x_lo
    m_here = x_hi * 2 + core
    a_out, b_out = [], []
    for j, (dy, other) in enumerate(PIECES):
        to_y = y_at(dy)
        to_core = core if other == 0 else 1 - core
        layer = to_y * 2 + to_core
        src = a_ref.at[pl.ds(layer * 4, 4)]
        dst = pa_ref.at[z, d_here]
        sem = a_recv.at[0, dy * 2 + apart]
        copy = remote(src, dst, a_send.at[j], sem, device(x_hi, core, to_core, to_y, z))
        if (dy, other) == (0, 0):
            stay = pltpu.make_async_copy(src, dst, sem)

            @pl.when(same)
            def _():
                stay.start()

            @pl.when(jnp.logical_not(same))
            def _():
                copy.start()

            first_out = copy
        else:
            copy.start()
            a_out.append(copy)
    copy = remote(c_ref, cs_ref, c_sem.at[0], c_sem.at[1], twin)
    copy.start()
    c_out = copy
    for j, (dy, other) in enumerate(PIECES):
        to_y = y_at(dy)
        to_core = core if other == 0 else 1 - core
        layer = to_y * 2 + to_core
        src = b_ref.at[pl.ds(layer * 4, 4)]
        dst = pb_ref.at[m_here, d_here]
        sem = b_recv.at[0, dy * 2 + other]
        if (dy, other) == (0, 0):
            pltpu.make_async_copy(src, dst, sem).start()
        else:
            copy = remote(src, dst, b_send.at[j], sem, device(x_hi, x_lo, to_core, to_y, z))
            copy.start()
            b_out.append(copy)

    def a_slot(back, dy, other):
        lo = x_lo if other == 0 else 1 - x_lo
        return pa_ref.at[lax.rem(z - back + 4, 4), y_at(-dy) * 2 + lo]

    def b_slot(back, dy, other):
        from_x = lax.rem(x - back + 4, 4)
        from_core = core if other == 0 else 1 - core
        return pb_ref.at[(from_x // 2) * 2 + from_core, y_at(-dy) * 2 + lax.rem(from_x, 2)]

    def turn(slot, recv, send, to, out, j):
        dy, other = PIECES[j]
        n = dy * 2 + other
        here = slot(0, dy, other)
        remote(here, here, send.at[0, n], recv.at[0, n], to(1)).wait_recv()
        for way, step in ((0, 1), (1, -1)):
            copy = remote(here, here, send.at[way, n], recv.at[1 if step == 1 else 3, n], to(step))
            copy.start()
            out.append(copy)

    def pass_on(slot, recv, send, to, out, j):
        dy, other = PIECES[j]
        n = dy * 2 + other
        back, step = (1, 1) if j % 2 == 0 else (3, -1)
        piece = slot(back, dy, other)
        remote(piece, piece, send.at[2, n], recv.at[back, n], to(step)).wait_recv()
        copy = remote(piece, piece, send.at[2, n], recv.at[2, n], to(step))
        copy.start()
        out.append(copy)

    a_args = (a_slot, a_recv, az_send, z_to, a_out)
    b_args = (b_slot, b_recv, bx_send, x_to, b_out)
    for entry in SCHEDULE:
        step = turn if entry[0] == "t" else pass_on
        step(*(a_args if entry[1] == "a" else b_args), int(entry[2]))
    for j, (dy, other) in enumerate(PIECES):
        n = dy * 2 + other
        for back in (3 if j % 2 == 0 else 1, 2):
            piece = a_slot(back, dy, other)
            remote(piece, piece, az_send.at[0, n], a_recv.at[back, n], z_to(1)).wait_recv()
            piece = b_slot(back, dy, other)
            remote(piece, piece, bx_send.at[0, n], b_recv.at[back, n], x_to(1)).wait_recv()
    for copy in a_out + b_out:
        copy.wait_send()
    c_out.wait()

    @pl.when(jnp.logical_not(same))
    def _():
        first_out.wait_send()


def gather_panels(a_local, b_local, c_pos):
    dma = pltpu.SemaphoreType.DMA
    return pl.pallas_call(
        gather_kernel,
        out_shape=(
            jax.ShapeDtypeStruct((4, 8, 4, 2, BS, BS), jnp.bfloat16),
            jax.ShapeDtypeStruct((4, 8, 4, BS, BS), jnp.bfloat16),
            jax.ShapeDtypeStruct(c_pos.shape, jnp.int32),
        ),
        in_specs=[ANY] * 3,
        out_specs=(ANY,) * 3,
        scratch_shapes=[
            dma((8,)), dma((4, 8)), dma((3, 8)), dma((8,)), dma((4, 8)), dma((3, 8)), dma((2,)),
        ],
        compiler_params=pltpu.CompilerParams(
            collective_id=0, has_side_effects=True, vmem_limit_bytes=60 * 2**20
        ),
        name="gather_panels",
    )(a_local, b_local, c_pos)


EXTRA = 4
NONE = 256 * 128


def product_kernel(
    rows_hbm, cols_hbm, mine_ref, twin_ref, pa_ref, pb_ref, out_ref,
    a_buf, b_buf, total, rows, cols, spots, jobs_v, jobs, extras, ends, sem,
):
    _, x_lo, core, _, _ = place()
    small = [
        pltpu.make_async_copy(rows_hbm, rows, sem.at[0]),
        pltpu.make_async_copy(cols_hbm, cols, sem.at[1]),
        pltpu.make_async_copy(mine_ref, spots.at[0], sem.at[2]),
        pltpu.make_async_copy(twin_ref, spots.at[1], sem.at[3]),
    ]
    loads = [
        pltpu.make_async_copy(pa_ref, a_buf.at[pl.ds(0, 256)], sem.at[4]),
        pltpu.make_async_copy(pb_ref, b_buf, sem.at[5]),
    ]
    for copy in small + loads:
        copy.start()
    a_buf[256] = jnp.zeros((BS, BS), jnp.bfloat16)
    for copy in small:
        copy.wait()

    spot = jnp.where(x_lo == core, spots[0, 0], spots[1, 0])
    kept_row = jnp.where(spot >= 0, spot // NBL, -2)
    kept_col = jnp.where(spot >= 0, spot % NBL, -2)
    k = lax.broadcasted_iota(jnp.int32, (16, BS), 0)
    a_base = (k % 4) * 64 + (k // 4) * 2
    b_base = (k % 4) * 32 + k // 4
    a_at = jnp.full((16, BS), -1, jnp.int32)
    b_at = jnp.full((16, BS), -1, jnp.int32)
    row_values, col_values = rows[...], cols[...]
    for u in range(16):
        a_at = jnp.where(row_values[:, u : u + 1] == kept_row, a_base + (u // 2 * 8 + u % 2), a_at)
    for v in range(8):
        b_at = jnp.where(col_values[:, v : v + 1] == kept_col, b_base + v * 4, b_at)
    code = jnp.where((a_at >= 0) & (b_at >= 0), a_at * 128 + b_at, NONE)

    found = [jnp.full((1, BS), NONE, jnp.int32) for _ in range(16)]
    count = jnp.zeros((1, BS), jnp.int32)
    for k in range(16):
        one = code[k : k + 1]
        live = one < NONE
        for j in range(k + 1):
            found[j] = jnp.where(live & (count == j), one, found[j])
        count = count + live.astype(jnp.int32)
    for j in range(16):
        jobs_v[j : j + 1] = found[j]
    jobs_v[16:17] = count
    jobs_v[18:20] = jnp.full((2, BS), NONE, jnp.int32)
    copy = pltpu.make_async_copy(jobs_v, jobs, sem.at[0])
    copy.start()
    copy.wait()

    def list_quarter(q, filled):
        def list_pairs(pair, filled):
            def one_slot(n, filled):
                slot = q * 32 + n
                extras[filled] = slot * 32 + pair * 2
                return filled + jnp.where(jobs[16, slot] > pair * 2, 1, 0)

            return lax.fori_loop(0, 32, one_slot, filled, unroll=8)

        def most(n, value):
            return jnp.maximum(value, jobs[16, q * 32 + n])

        pairs = (lax.fori_loop(0, 32, most, 0, unroll=8) + 1) // 2
        filled = lax.fori_loop(1, pairs, list_pairs, filled)
        for n in range(EXTRA - 1):
            extras[filled + n] = q * 1024 + 18
        filled = (filled + EXTRA - 1) // EXTRA * EXTRA
        ends[q + 1] = filled
        return filled

    ends[0] = 0
    lax.fori_loop(0, 4, list_quarter, 0)
    for load in loads:
        load.wait()

    def pair_product(first, second):
        left = jnp.concatenate([a_buf[first // 128], a_buf[second // 128]], axis=1)
        right = jnp.concatenate([b_buf[first % 128], b_buf[second % 128]], axis=0)
        return jnp.dot(left, right, preferred_element_type=jnp.float32)

    def quarter(q, _):
        def some_slots(n, _):
            for s in range(8):
                slot = q * 32 + n * 8 + s
                total[slot] = pair_product(jobs[0, slot], jobs[1, slot])
            return 0

        lax.fori_loop(0, 4, some_slots, 0)

        def some_extras(n, _):
            entries = [extras[n * EXTRA + e] for e in range(EXTRA)]
            terms = [
                pair_product(jobs[entry % 32, entry // 32], jobs[entry % 32 + 1, entry // 32])
                for entry in entries
            ]
            for entry, term in zip(entries, terms):
                total[entry // 32] += term
            return 0

        lax.fori_loop(ends[q] // EXTRA, ends[q + 1] // EXTRA, some_extras, 0)
        span = pl.ds(q * 32, 32)
        pltpu.make_async_copy(total.at[span], out_ref.at[span], sem.at[q]).start()
        return 0

    lax.fori_loop(0, 4, quarter, 0)
    for q in range(4):
        span = pl.ds(q * 32, 32)
        pltpu.make_async_copy(total.at[span], out_ref.at[span], sem.at[q]).wait()


def partial_sums(rows, cols, mine, twin, panel_a, panel_b):
    i32 = jnp.int32
    return pl.pallas_call(
        product_kernel,
        out_shape=jax.ShapeDtypeStruct((BS, BS, BS), jnp.float32),
        in_specs=[ANY] * 6,
        out_specs=ANY,
        scratch_shapes=[
            pltpu.VMEM((257, BS, BS), jnp.bfloat16),
            pltpu.VMEM((128, BS, BS), jnp.bfloat16),
            pltpu.VMEM((BS, BS, BS), jnp.float32),
            pltpu.VMEM(rows.shape, i32),
            pltpu.VMEM(cols.shape, i32),
            pltpu.VMEM((2,) + mine.shape, i32),
            pltpu.VMEM((24, BS), i32),
            pltpu.SMEM((24, BS), i32),
            pltpu.SMEM((1024,), i32),
            pltpu.SMEM((8,), i32),
            pltpu.SemaphoreType.DMA((6,)),
        ],
        compiler_params=pltpu.CompilerParams(vmem_limit_bytes=60 * 2**20),
        name="partial_sums",
    )(rows, cols, mine, twin, panel_a, panel_b)


TOP = 32767.0
TINY = 2e-34
HALF = 8


def reduce_kernel(
    part_ref, out_ref, own, other, done_ref, q_out, s_out, q_in, s_in,
    load_sem, twin_sem, q_send, q_recv, s_send, s_recv, out_sem,
):
    x_hi, x_lo, core, y, z = place()
    same = x_lo == core

    def y_at(step):
        return lax.rem(y + step + 4, 4)

    def y_to(step):
        return device(x_hi, x_lo, core, y_at(step), z)

    twin = device(x_hi, x_lo, 1 - core, y, z)
    owner = device(x_hi, core, x_lo, y, z)

    barrier = pltpu.get_barrier_semaphore()

    def greet(to):
        pl.semaphore_signal(barrier, inc=1, device_id=to, device_id_type=MESH)

    greet(twin)
    greet(y_to(1))
    greet(y_to(-1))

    @pl.when(jnp.logical_not(same))
    def _():
        greet(owner)

    loads, twins, sent = {}, {}, []
    order = (2, 1, 3, 0)
    for r in order:
        loads[r] = pltpu.make_async_copy(part_ref.at[y_at(r), core], own.at[r], load_sem.at[r])
        loads[r].start()
    pl.semaphore_wait(barrier, 3 + jnp.where(same, 0, 1))
    for r in order:
        twins[r] = remote(
            part_ref.at[y_at(r), 1 - core], other.at[r], twin_sem.at[0, r], twin_sem.at[1, r], twin
        )
        twins[r].start()

    def meet(r):
        loads[r].wait()
        twins[r].wait_recv()

    def arrived(i):
        remote(q_in.at[i], q_in.at[i], q_send.at[i], q_recv.at[i], twin).wait_recv()
        remote(s_in.at[i], s_in.at[i], s_send.at[i], s_recv.at[i], twin).wait_recv()

    def chip_sum(r, slot):
        return own[r, slot] + other[r, slot]

    def value(i, n):
        return q_in[i, n].astype(jnp.float32) * s_in[i, pl.ds(n, 1)]

    def pass_on(i, step, r, first, plus=None):
        def one(n, _):
            sums = chip_sum(r, first + n)
            if plus is not None:
                sums = sums + value(plus, n)
            top = jnp.maximum(jnp.max(jnp.abs(sums), axis=0, keepdims=True), TINY)
            q_out[i, n] = jnp.round(sums * (TOP / top)).astype(jnp.int32).astype(jnp.int16)
            s_out[i, pl.ds(n, 1)] = top * (1 / TOP)
            return 0

        lax.fori_loop(0, HALF, one, 0)
        for src, dst, send, recv in ((q_out, q_in, q_send, q_recv), (s_out, s_in, s_send, s_recv)):
            copy = remote(src.at[i], dst.at[i], send.at[i], recv.at[i], y_to(step))
            copy.start()
            sent.append(copy)

    meet(2)
    pass_on(0, 1, 2, 0)
    pass_on(1, -1, 2, HALF)
    meet(1)
    pass_on(2, 1, 1, HALF)
    meet(3)
    pass_on(3, -1, 3, 0)
    arrived(0)
    pass_on(4, 1, 1, 0, plus=0)
    arrived(1)
    pass_on(5, -1, 3, HALF, plus=1)
    meet(0)

    def finish(half, first, second):
        def one(n, _):
            slot = half * HALF + n
            sums = chip_sum(0, slot) + value(first, n) + value(second, n)
            done_ref[slot] = sums.astype(jnp.bfloat16)
            return 0

        lax.fori_loop(0, HALF, one, 0)
        span = pl.ds(half * HALF, HALF)

        @pl.when(same)
        def _():
            pltpu.make_async_copy(done_ref.at[span], out_ref.at[span], out_sem.at[1, half]).start()

        @pl.when(jnp.logical_not(same))
        def _():
            remote(
                done_ref.at[span], out_ref.at[span], out_sem.at[0, half], out_sem.at[1, half], owner
            ).start()

    arrived(3)
    arrived(4)
    finish(0, 3, 4)
    arrived(2)
    arrived(5)
    finish(1, 2, 5)
    for half in range(2):
        span = pl.ds(half * HALF, HALF)
        copy = remote(done_ref.at[span], out_ref.at[span], out_sem.at[0, half], out_sem.at[1, half], owner)
        copy.wait_recv()

        @pl.when(jnp.logical_not(same))
        def _():
            copy.wait_send()

    for copy in sent:
        copy.wait_send()
    for r in order:
        twins[r].wait_send()


def reduce_sums(part):
    dma = pltpu.SemaphoreType.DMA
    f32 = jnp.float32
    return pl.pallas_call(
        reduce_kernel,
        out_shape=jax.ShapeDtypeStruct((16, BS, BS), jnp.bfloat16),
        in_specs=[ANY],
        out_specs=pl.BlockSpec(memory_space=pltpu.VMEM),
        scratch_shapes=[
            pltpu.VMEM((4, 16, BS, BS), f32),
            pltpu.VMEM((4, 16, BS, BS), f32),
            pltpu.VMEM((16, BS, BS), jnp.bfloat16),
            pltpu.VMEM((6, HALF, BS, BS), jnp.int16),
            pltpu.VMEM((6, HALF, BS), f32),
            pltpu.VMEM((6, HALF, BS, BS), jnp.int16),
            pltpu.VMEM((6, HALF, BS), f32),
            dma((4,)), dma((2, 4)), dma((6,)), dma((6,)), dma((6,)), dma((6,)), dma((2, 2)),
        ],
        compiler_params=pltpu.CompilerParams(
            collective_id=1, has_side_effects=True, vmem_limit_bytes=60 * 2**20
        ),
        name="reduce_sums",
    )(part)


def per_device(a_blocks, a_rows, b_blocks, b_cols, c_pos):
    x_hi, x_lo, core, y, z = place()
    layer = y * 2 + core
    rows = lax.dynamic_slice(a_rows, (layer * 4, 0, x_hi * 2 + x_lo, 0), (4, 4, 1, 16)).reshape(16, 16)
    cols = lax.dynamic_slice(b_cols, (layer * 4, 0, z, 0), (4, 4, 1, 8)).reshape(16, 8)
    panel_a, panel_b, twin_pos = gather_panels(a_blocks[:, 0, 0], b_blocks[:, 0, 0, 0], c_pos)
    part = partial_sums(
        rows, cols, c_pos, twin_pos, panel_a.reshape(256, BS, BS), panel_b.reshape(128, BS, BS)
    )
    return reduce_sums(part.reshape(4, 2, 16, BS, BS))[None, None]


def solution(mesh):
    placed = (
        P(None, "col", "row", "depth", None, None),
        P(),
        P(None, "row", "col", "depth", None, None),
        P(),
        P("row", "col", None),
    )
    return jax.shard_map(
        per_device,
        mesh=mesh,
        in_specs=placed,
        out_specs=P("row", "col", "depth", None, None),
        check_vma=False,
    )
```

```python
import jax
import jax.numpy as jnp
from jax import lax
from jax.experimental import pallas as pl
from jax.experimental.pallas import tpu as pltpu
from jax.sharding import PartitionSpec as P

MESH = pl.DeviceIdType.MESH
BS = 128
NBL = 16
ANY = pl.BlockSpec(memory_space=pl.ANY)


def place():
    row, z, depth = lax.axis_index("row"), lax.axis_index("col"), lax.axis_index("depth")
    return row // 2, depth % 2, row % 2, depth // 2, z


def device(x_hi, x_lo, core, y, z):
    return (x_hi * 2 + core, z, y * 2 + x_lo)


def remote(src, dst, send, recv, to):
    return pltpu.make_async_remote_copy(
        src_ref=src, dst_ref=dst, send_sem=send, recv_sem=recv, device_id=to, device_id_type=MESH
    )


STEPS = (0, 1, 3, 2)
TOP = 32767.0
TINY = 2e-34
HALF = 8
ZERO = 32
NONE = ZERO * 64


def kernel(
    a_ref, b_ref, c_ref, rows_ref, cols_ref, out_ref,
    a00, a01, a02, a03, a10, a11, a12, a13, b0, b1, spots, codes, jobs, total, other, done, q_out, s_out, q_in, s_in,
    az_out, az_recv, az_ring, az_got, bx_out, bx_recv, bx_ring, bx_got, c_sem,
    twin_sem, q_send, q_recv, s_send, s_recv, out_sem,
):
    x_hi, x_lo, core, y, z = place()
    x = x_hi * 2 + x_lo
    same = x_lo == core
    apart = jnp.where(same, 0, 1)
    a_half, b_half = ((a00, a01, a02, a03), (a10, a11, a12, a13)), (b0, b1)

    def turned(at, step):
        return lax.rem(at + step + 8, 4)

    def differ(at, flag):
        return at if flag == 0 else 1 - at

    def z_to(step):
        return device(x_hi, x_lo, core, y, turned(z, step))

    def x_to(step):
        to = turned(x, step)
        return device(to // 2, lax.rem(to, 2), core, y, z)

    def y_to(step):
        return device(x_hi, x_lo, core, turned(y, step), z)

    twin = device(x_hi, x_lo, 1 - core, y, z)
    owner = device(x_hi, core, x_lo, y, z)

    barrier = pltpu.get_barrier_semaphore()

    def greet(to):
        pl.semaphore_signal(barrier, inc=1, device_id=to, device_id_type=MESH)

    for dy in STEPS:
        for flag in range(2):
            if (dy, flag) == (0, 0):

                @pl.when(jnp.logical_not(same))
                def _():
                    greet(twin)

            else:
                greet(device(x_hi, differ(x_lo, flag), x_lo, turned(y, -dy), z))
                greet(device(x_hi, x_lo, differ(core, flag), turned(y, -dy), z))
    for step in (1, -1):
        greet(z_to(step))
        greet(x_to(step))
    pl.semaphore_wait(barrier, 18 + apart)

    waits = []

    def send(src, dst, sent, recv, to):
        copy = remote(src, dst, sent, recv, to)
        copy.start()
        waits.append(copy.wait_send)

    def landed(piece, recv):
        remote(piece, piece, recv, recv, twin).wait_recv()

    def a_piece(half, back, at_y, at_lo):
        return a_half[half][back].at[pl.ds(at_y * 8 + at_lo * 4, 4)]

    def a_pieces(half, back, at_y):
        return a_half[half][back].at[pl.ds(at_y * 8, 8)]

    def b_piece(half, at_x, at_y, at_core):
        return b_half[half].at[pl.ds(at_x * 16 + at_y * 4 + at_core * 2, 2)]

    def b_pieces(half, at_x, at_y):
        return b_half[half].at[pl.ds(at_x * 16 + at_y * 4, 4)]

    def hand_out(half):
        for n, dy in enumerate(STEPS):
            for flag in range(2):
                to_y, to_core = turned(y, dy), differ(core, flag)
                group = (to_y * 2 + to_core) * 4 + half * 2
                src, dst = a_ref.at[pl.ds(group * 2, 4)], a_piece(half, 0, y, x_lo)
                sent, recv = az_out.at[half, n * 2 + flag], az_recv.at[half, n * 2 + apart]
                to = device(x_hi, core, to_core, to_y, z)
                if (dy, flag) == (0, 0):
                    hand_out_here(src, dst, sent, recv, to)
                else:
                    send(src, dst, sent, recv, to)
        for n, dy in enumerate(STEPS):
            for flag in range(2):
                to_y, to_core = turned(y, dy), differ(core, flag)
                group = (to_y * 2 + to_core) * 4 + half * 2
                src, dst = b_ref.at[pl.ds(group, 2)], b_piece(half, x, y, core)
                sent, recv = bx_out.at[half, n * 2 + flag], bx_recv.at[half, n * 2 + flag]
                if (dy, flag) == (0, 0):
                    pltpu.make_async_copy(src, dst, recv).start()
                else:
                    send(src, dst, sent, recv, device(x_hi, x_lo, to_core, to_y, z))

    def hand_out_here(src, dst, sent, recv, to):
        copy = remote(src, dst, sent, recv, to)
        stay = pltpu.make_async_copy(src, dst, recv)
        pl.when(same)(lambda: stay.start())
        pl.when(jnp.logical_not(same))(lambda: copy.start())
        waits.append(lambda: pl.when(jnp.logical_not(same))(lambda: copy.wait_send()))

    def turn_a(half, n):
        at = turned(y, -STEPS[n])
        for flag in range(2):
            landed(a_piece(half, 0, at, differ(x_lo, flag)), az_recv.at[half, n * 2 + flag])
        for back, step in ((1, 1), (3, -1)):
            send(
                a_pieces(half, 0, at), a_pieces(half, back, at), az_ring.at[half, back, n],
                az_got.at[half, back, n], z_to(step),
            )

    def pass_a(half, n):
        at = turned(y, -STEPS[n])
        back, step = (1, 1) if n % 2 == 0 else (3, -1)
        landed(a_pieces(half, back, at), az_got.at[half, back, n])
        send(
            a_pieces(half, back, at), a_pieces(half, 2, at), az_ring.at[half, 2, n], az_got.at[half, 2, n],
            z_to(step),
        )

    def rest_a(half, back):
        for n in range(4):
            if back == 2 or back != (1 if n % 2 == 0 else 3):
                landed(a_pieces(half, back, turned(y, -STEPS[n])), az_got.at[half, back, n])

    def turn_b(half, n):
        at = turned(y, -STEPS[n])
        for flag in range(2):
            landed(b_piece(half, x, at, differ(core, flag)), bx_recv.at[half, n * 2 + flag])
        here = b_pieces(half, x, at)
        for back, step in ((1, 1), (3, -1)):
            send(here, here, bx_ring.at[half, back, n], bx_got.at[half, back, n], x_to(step))

    def pass_b(half, n):
        back, step = (1, 1) if n % 2 == 0 else (3, -1)
        there = b_pieces(half, turned(x, -back), turned(y, -STEPS[n]))
        landed(there, bx_got.at[half, back, n])
        send(there, there, bx_ring.at[half, 2, n], bx_got.at[half, 2, n], x_to(step))

    def rest_b(half):
        for n in range(4):
            for back in (3 if n % 2 == 0 else 1, 2):
                landed(b_pieces(half, turned(x, -back), turned(y, -STEPS[n])), bx_got.at[half, back, n])

    def pair_up():
        landed(spots.at[1], c_sem.at[1])
        spot = jnp.where(same, c_ref[0], spots[1, 0])
        kept_row = jnp.where(spot >= 0, spot // NBL, -2)
        kept_col = jnp.where(spot >= 0, spot % NBL, -2)
        k = lax.broadcasted_iota(jnp.int32, (16, BS), 0)
        group, m = (k // 4) % 2, k % 4
        a_at = jnp.full((16, BS), -1, jnp.int32)
        b_at = jnp.full((16, BS), -1, jnp.int32)
        row_values, col_values = rows_ref[...], cols_ref[...]
        for u in range(16):
            a_at = jnp.where(row_values[:, u : u + 1] == kept_row, group * 2 + (u // 2 * 4 + u % 2), a_at)
        b_base = (m // 2) * 32 + (m % 2) * 2 + group
        for v in range(8):
            b_at = jnp.where(col_values[:, v : v + 1] == kept_col, b_base + (v % 2 * 16 + v // 2 * 4), b_at)
        codes[...] = jnp.where((a_at >= 0) & (b_at >= 0), a_at * 64 + b_at, NONE)
        copy = pltpu.make_async_copy(codes, jobs, c_sem.at[2])
        copy.start()
        copy.wait()

    def add_products(half, back, first, count, fresh=False):
        left_ref, right_ref = a_half[half][back], b_half[half]
        k = half * 8 + turned(z, -back)

        def some(n, _):
            for s in range(32):
                slot = first + n * 32 + s
                one, two = jobs[k, slot], jobs[k + 4, slot]
                left = jnp.concatenate([left_ref[one >> 6], left_ref[two >> 6]], axis=1)
                right = jnp.concatenate([right_ref[one & 63], right_ref[two & 63]], axis=0)
                term = jnp.dot(left, right, preferred_element_type=jnp.float32)
                if fresh:
                    total[slot] = term
                else:
                    total[slot] += term
            return 0

        lax.fori_loop(0, count // 32, some, 0)

    hand_out(0)
    send(c_ref, spots.at[1], c_sem.at[0], c_sem.at[1], twin)
    for half in a_half:
        for ref in half:
            ref[ZERO] = jnp.zeros((BS, BS), jnp.bfloat16)
    turn_a(0, 0)
    turn_b(0, 0)
    turn_a(0, 1)
    pass_a(0, 0)
    turn_a(0, 2)
    pass_a(0, 1)
    turn_a(0, 3)
    turn_b(0, 1)
    turn_b(0, 2)
    hand_out(1)
    turn_b(0, 3)
    pass_a(0, 2)
    pass_b(0, 0)
    pass_b(0, 1)
    pass_a(0, 3)
    pass_b(0, 2)
    pass_b(0, 3)
    pair_up()
    for n in range(4):
        turn_a(1, n)
    turn_b(1, 0)
    turn_b(1, 1)
    rest_b(0)
    add_products(0, 0, 0, BS, fresh=True)
    turn_b(1, 2)
    turn_b(1, 3)
    rest_a(0, 1)
    add_products(0, 1, 0, BS)
    pass_a(1, 0)
    pass_b(1, 0)
    pass_b(1, 1)
    rest_a(0, 3)
    add_products(0, 3, 0, BS)
    pass_a(1, 1)
    pass_b(1, 2)
    pass_b(1, 3)
    rest_a(0, 2)
    add_products(0, 2, 0, BS)
    pass_a(1, 2)
    rest_b(1)
    add_products(1, 0, 0, BS)
    pass_a(1, 3)
    rest_a(1, 1)
    add_products(1, 1, 0, BS)
    rest_a(1, 3)
    add_products(1, 3, 0, BS)
    rest_a(1, 2)

    def start_of(r):
        return turned(y, r) * 32

    for r in (2, 1, 3, 0):
        add_products(1, 2, start_of(r), 32)
        send(
            total.at[pl.ds(start_of(r) + (1 - core) * 16, 16)], other.at[r], twin_sem.at[0, r],
            twin_sem.at[1, r], twin,
        )

    def meet(r):
        landed(other.at[r], twin_sem.at[1, r])

    def arrived(i):
        landed(q_in.at[i], q_recv.at[i])
        landed(s_in.at[i], s_recv.at[i])

    def chip_sum(r, slot):
        return total[start_of(r) + core * 16 + slot] + other[r, slot]

    def value(i, n):
        return q_in[i, n].astype(jnp.float32) * s_in[i, pl.ds(n, 1)]

    def tell(i, step, r, first, plus=None):
        def one(n, _):
            sums = chip_sum(r, first + n)
            if plus is not None:
                sums = sums + value(plus, n)
            top = jnp.maximum(jnp.max(jnp.abs(sums), axis=0, keepdims=True), TINY)
            q_out[i, n] = jnp.round(sums * (TOP / top)).astype(jnp.int32).astype(jnp.int16)
            s_out[i, pl.ds(n, 1)] = top * (1 / TOP)
            return 0

        lax.fori_loop(0, HALF, one, 0)
        send(q_out.at[i], q_in.at[i], q_send.at[i], q_recv.at[i], y_to(step))
        send(s_out.at[i], s_in.at[i], s_send.at[i], s_recv.at[i], y_to(step))

    meet(2)
    tell(0, 1, 2, 0)
    tell(1, -1, 2, HALF)
    meet(1)
    tell(2, 1, 1, HALF)
    meet(3)
    tell(3, -1, 3, 0)
    arrived(0)
    tell(4, 1, 1, 0, plus=0)
    arrived(1)
    tell(5, -1, 3, HALF, plus=1)
    meet(0)

    def finish(half, first, second):
        def one(n, _):
            slot = half * HALF + n
            sums = chip_sum(0, slot) + value(first, n) + value(second, n)
            done[slot] = sums.astype(jnp.bfloat16)
            return 0

        lax.fori_loop(0, HALF, one, 0)
        span = pl.ds(half * HALF, HALF)
        hand_out_here(done.at[span], out_ref.at[span], out_sem.at[0, half], out_sem.at[1, half], owner)

    arrived(3)
    arrived(4)
    finish(0, 3, 4)
    arrived(2)
    arrived(5)
    finish(1, 2, 5)
    for half in range(2):
        landed(out_ref.at[pl.ds(half * HALF, HALF)], out_sem.at[1, half])
    for wait in waits:
        wait()


def per_device(a_blocks, a_rows, b_blocks, b_cols, c_pos):
    x_hi, x_lo, core, y, z = place()
    layer = y * 2 + core
    rows = lax.dynamic_slice(a_rows, (layer * 4, 0, x_hi * 2 + x_lo, 0), (4, 4, 1, 16)).reshape(16, 16)
    cols = lax.dynamic_slice(b_cols, (layer * 4, 0, z, 0), (4, 4, 1, 8)).reshape(16, 8)
    dma = pltpu.SemaphoreType.DMA
    vmem = pl.BlockSpec(memory_space=pltpu.VMEM)
    bf16, f32, i16, i32 = jnp.bfloat16, jnp.float32, jnp.int16, jnp.int32
    out = pl.pallas_call(
        kernel,
        out_shape=jax.ShapeDtypeStruct((16, BS, BS), bf16),
        in_specs=[ANY, ANY, vmem, vmem, vmem],
        out_specs=vmem,
        scratch_shapes=[
            *[pltpu.VMEM((ZERO + 1, BS, BS), bf16)] * 8,
            *[pltpu.VMEM((64, BS, BS), bf16)] * 2,
            pltpu.VMEM((2,) + c_pos.shape, i32),
            pltpu.VMEM((16, BS), i32),
            pltpu.SMEM((16, BS), i32),
            pltpu.VMEM((BS, BS, BS), f32),
            pltpu.VMEM((4, 16, BS, BS), f32),
            pltpu.VMEM((16, BS, BS), bf16),
            pltpu.VMEM((6, HALF, BS, BS), i16),
            pltpu.VMEM((6, HALF, BS), f32),
            pltpu.VMEM((6, HALF, BS, BS), i16),
            pltpu.VMEM((6, HALF, BS), f32),
            dma((2, 8)), dma((2, 8)), dma((2, 4, 4)), dma((2, 4, 4)),
            dma((2, 8)), dma((2, 8)), dma((2, 4, 4)), dma((2, 4, 4)), dma((3,)),
            dma((2, 4)), dma((6,)), dma((6,)), dma((6,)), dma((6,)), dma((2, 2)),
        ],
        compiler_params=pltpu.CompilerParams(
            collective_id=0, has_side_effects=True, vmem_limit_bytes=60 * 2**20
        ),
        name="block_product",
    )(a_blocks.reshape(64, BS, BS), b_blocks.reshape(32, BS, BS), c_pos, rows, cols)
    return out[None, None]


def solution(mesh):
    placed = (
        P(None, "col", "row", "depth", None, None),
        P(),
        P(None, "row", "col", "depth", None, None),
        P(),
        P("row", "col", None),
    )
    return jax.shard_map(
        per_device,
        mesh=mesh,
        in_specs=placed,
        out_specs=P("row", "col", "depth", None, None),
        check_vma=False,
    )
```

```python
import jax
import jax.numpy as jnp
from jax import lax
from jax.experimental import pallas as pl
from jax.experimental.pallas import tpu as pltpu
from jax.sharding import PartitionSpec as P

MESH = pl.DeviceIdType.MESH
BS = 128
NBL = 16
ANY = pl.BlockSpec(memory_space=pl.ANY)


def place():
    row, z, depth = lax.axis_index("row"), lax.axis_index("col"), lax.axis_index("depth")
    return row // 2, depth % 2, row % 2, depth // 2, z


def device(x_hi, x_lo, core, y, z):
    return (x_hi * 2 + core, z, y * 2 + x_lo)


def remote(src, dst, send, recv, to):
    return pltpu.make_async_remote_copy(
        src_ref=src, dst_ref=dst, send_sem=send, recv_sem=recv, device_id=to, device_id_type=MESH
    )


STEPS = (0, 1, 3, 2)
UNITS = ((0, 0), (0, 1), (1, None), (2, None), (3, 0), (3, 1))
TOP = 32767.0
TINY = 2e-34
PART = 4
ZERO = 32
NONE = ZERO * 64


def kernel(
    a_ref, b_ref, c_ref, rows_ref, cols_ref, out_ref,
    a00, a01, a02, a03, a10, a11, a12, a13, b0, b1, spots, rows, cols, codes, jobs, total, other, done, q_out, s_out, q_in, s_in,
    az_out, az_recv, az_ring, az_got, bx_out, bx_recv, bx_ring, bx_got, c_sem,
    twin_sem, q_send, q_recv, s_send, s_recv, out_sem,
):
    x_hi, x_lo, core, y, z = place()
    x = x_hi * 2 + x_lo
    same = x_lo == core
    apart = jnp.where(same, 0, 1)
    a_half, b_half = ((a00, a01, a02, a03), (a10, a11, a12, a13)), (b0, b1)

    def turned(at, step):
        return lax.rem(at + step + 8, 4)

    def differ(at, flag):
        return at if flag == 0 else 1 - at

    def z_to(step):
        return device(x_hi, x_lo, core, y, turned(z, step))

    def x_to(step):
        to = turned(x, step)
        return device(to // 2, lax.rem(to, 2), core, y, z)

    def y_to(step):
        return device(x_hi, x_lo, core, turned(y, step), z)

    twin = device(x_hi, x_lo, 1 - core, y, z)
    owner = device(x_hi, core, x_lo, y, z)

    barrier = pltpu.get_barrier_semaphore()

    def greet(to):
        pl.semaphore_signal(barrier, inc=1, device_id=to, device_id_type=MESH)

    for dy in STEPS:
        for flag in range(2):
            if (dy, flag) == (0, 0):

                @pl.when(jnp.logical_not(same))
                def _():
                    greet(twin)

            else:
                greet(device(x_hi, differ(x_lo, flag), x_lo, turned(y, -dy), z))
                greet(device(x_hi, x_lo, differ(core, flag), turned(y, -dy), z))
    for step in (1, -1):
        greet(z_to(step))
        greet(x_to(step))
    pl.semaphore_wait(barrier, 18 + apart)

    waits = []

    def send(src, dst, sent, recv, to):
        copy = remote(src, dst, sent, recv, to)
        copy.start()
        waits.append(copy.wait_send)

    def landed(piece, recv):
        remote(piece, piece, recv, recv, twin).wait_recv()

    def a_piece(half, back, at_y, at_lo):
        return a_half[half][back].at[pl.ds(at_y * 8 + at_lo * 4, 4)]

    def a_pieces(half, back, at_y):
        return a_half[half][back].at[pl.ds(at_y * 8, 8)]

    def b_piece(half, at_x, at_y, at_core):
        return b_half[half].at[pl.ds(at_x * 16 + at_y * 4 + at_core * 2, 2)]

    def b_pieces(half, at_x, at_y):
        return b_half[half].at[pl.ds(at_x * 16 + at_y * 4, 4)]

    def hand_out(half):
        for n, dy in enumerate(STEPS):
            for flag in range(2):
                to_y, to_core = turned(y, dy), differ(core, flag)
                group = (to_y * 2 + to_core) * 4 + half * 2
                src, dst = a_ref.at[pl.ds(group * 2, 4)], a_piece(half, 0, y, x_lo)
                sent, recv = az_out.at[half, n * 2 + flag], az_recv.at[half, n * 2 + apart]
                to = device(x_hi, core, to_core, to_y, z)
                if (dy, flag) == (0, 0):
                    hand_out_here(src, dst, sent, recv, to)
                else:
                    send(src, dst, sent, recv, to)
        for n, dy in enumerate(STEPS):
            for flag in range(2):
                to_y, to_core = turned(y, dy), differ(core, flag)
                group = (to_y * 2 + to_core) * 4 + half * 2
                src, dst = b_ref.at[pl.ds(group, 2)], b_piece(half, x, y, core)
                sent, recv = bx_out.at[half, n * 2 + flag], bx_recv.at[half, n * 2 + flag]
                if (dy, flag) == (0, 0):
                    pltpu.make_async_copy(src, dst, recv).start()
                else:
                    send(src, dst, sent, recv, device(x_hi, x_lo, to_core, to_y, z))

    def hand_out_here(src, dst, sent, recv, to):
        copy = remote(src, dst, sent, recv, to)
        stay = pltpu.make_async_copy(src, dst, recv)
        pl.when(same)(lambda: stay.start())
        pl.when(jnp.logical_not(same))(lambda: copy.start())
        waits.append(lambda: pl.when(jnp.logical_not(same))(lambda: copy.wait_send()))

    def a_unit(half, back, i):
        n, flag = UNITS[i]
        at = turned(y, -STEPS[n])
        return a_pieces(half, back, at) if flag is None else a_piece(half, back, at, differ(x_lo, flag))

    def turn_a(half, i):
        n, flag = UNITS[i]
        for one in range(2) if flag is None else (flag,):
            piece = a_piece(half, 0, turned(y, -STEPS[n]), differ(x_lo, one))
            landed(piece, az_recv.at[half, n * 2 + one])
        for back, step in ((1, 1), (3, -1)):
            send(
                a_unit(half, 0, i), a_unit(half, back, i), az_ring.at[half, back, i], az_got.at[half, back, i],
                z_to(step),
            )

    def pass_a(half, i):
        back, step = (1, 1) if i % 2 == 0 else (3, -1)
        landed(a_unit(half, back, i), az_got.at[half, back, i])
        send(
            a_unit(half, back, i), a_unit(half, 2, i), az_ring.at[half, 2, i], az_got.at[half, 2, i], z_to(step)
        )

    def rest_a(half, back):
        for i in range(len(UNITS)):
            if back == 2 or back != (1 if i % 2 == 0 else 3):
                landed(a_unit(half, back, i), az_got.at[half, back, i])

    def turn_b(half, n):
        at = turned(y, -STEPS[n])
        for flag in range(2):
            landed(b_piece(half, x, at, differ(core, flag)), bx_recv.at[half, n * 2 + flag])
        here = b_pieces(half, x, at)
        for back, step in ((1, 1), (3, -1)):
            send(here, here, bx_ring.at[half, back, n], bx_got.at[half, back, n], x_to(step))

    def pass_b(half, n):
        back, step = (1, 1) if n % 2 == 0 else (3, -1)
        there = b_pieces(half, turned(x, -back), turned(y, -STEPS[n]))
        landed(there, bx_got.at[half, back, n])
        send(there, there, bx_ring.at[half, 2, n], bx_got.at[half, 2, n], x_to(step))

    def rest_b(half):
        for n in range(4):
            for back in (3 if n % 2 == 0 else 1, 2):
                landed(b_pieces(half, turned(x, -back), turned(y, -STEPS[n])), bx_got.at[half, back, n])

    def pair_up():
        for copy in index_copies:
            copy.wait()
        landed(spots.at[1], c_sem.at[1])
        spot = jnp.where(same, spots[0, 0], spots[1, 0])
        kept_row = jnp.where(spot >= 0, spot // NBL, -2)
        kept_col = jnp.where(spot >= 0, spot % NBL, -2)

        def number_of(index, kept, number):
            slots, groups = index.shape

            def one(g):
                lane = lax.broadcasted_iota(jnp.int32, (slots, groups), 1)
                mine = jnp.sum(jnp.where(lane == g, index, 0), axis=1, keepdims=True)
                return jnp.max(jnp.where(mine == kept, number, -1), axis=0, keepdims=True)

            return one

        u = lax.broadcasted_iota(jnp.int32, (16, BS), 0)
        v = lax.broadcasted_iota(jnp.int32, (8, BS), 0)
        for m in range(4):
            row_of = number_of(rows[m], kept_row, (u >> 1) * 4 + (u & 1))
            col_of = number_of(cols[m], kept_col, (v & 1) * 16 + (v >> 1) * 4)
            for n in range(4):
                a_at, b_at = row_of((y * 2 + core) * 4 + n), col_of((y * 2 + core) * 4 + n)
                code = (a_at + n % 2 * 2) * 64 + b_at + (m // 2 * 32 + m % 2 * 2 + n % 2)
                codes[n * 4 + m : n * 4 + m + 1] = jnp.where((a_at >= 0) & (b_at >= 0), code, NONE)
        copy = pltpu.make_async_copy(codes, jobs, c_sem.at[2])
        copy.start()
        copy.wait()

    def add_products(half, back, first, count, fresh=False):
        left_ref, right_ref = a_half[half][back], b_half[half]
        k = half * 8 + turned(z, -back)

        def some(n, _):
            for s in range(32):
                slot = first + n * 32 + s
                one, two = jobs[k, slot], jobs[k + 4, slot]
                left = jnp.concatenate([left_ref[one >> 6], left_ref[two >> 6]], axis=1)
                right = jnp.concatenate([right_ref[one & 63], right_ref[two & 63]], axis=0)
                term = jnp.dot(left, right, preferred_element_type=jnp.float32)
                if fresh:
                    total[slot] = term
                else:
                    total[slot] += term
            return 0

        lax.fori_loop(0, count // 32, some, 0)

    hand_out(0)
    send(c_ref, spots.at[1], c_sem.at[0], c_sem.at[1], twin)
    index_copies = [
        pltpu.make_async_copy(c_ref, spots.at[0], c_sem.at[2]),
        pltpu.make_async_copy(rows_ref.at[:, x], rows, c_sem.at[3]),
        pltpu.make_async_copy(cols_ref.at[:, z], cols, c_sem.at[4]),
    ]
    for copy in index_copies:
        copy.start()
    for half in a_half:
        for ref in half:
            ref[ZERO] = jnp.zeros((BS, BS), jnp.bfloat16)
    turn_a(0, 0)
    turn_a(0, 1)
    turn_b(0, 0)
    turn_a(0, 2)
    pass_a(0, 0)
    pass_a(0, 1)
    turn_a(0, 3)
    pass_a(0, 2)
    turn_a(0, 4)
    turn_a(0, 5)
    turn_b(0, 1)
    turn_b(0, 2)
    hand_out(1)
    turn_b(0, 3)
    pass_a(0, 3)
    pass_b(0, 0)
    pass_b(0, 1)
    pass_a(0, 4)
    pass_a(0, 5)
    pass_b(0, 2)
    pass_b(0, 3)
    pair_up()
    turn_a(1, 0)
    turn_a(1, 1)
    turn_a(1, 2)
    turn_a(1, 3)
    turn_a(1, 4)
    turn_a(1, 5)
    turn_b(1, 0)
    turn_b(1, 1)
    rest_b(0)
    add_products(0, 0, 0, BS, fresh=True)
    turn_b(1, 2)
    turn_b(1, 3)
    rest_a(0, 1)
    add_products(0, 1, 0, BS)
    pass_a(1, 0)
    pass_a(1, 1)
    pass_b(1, 0)
    pass_b(1, 1)
    rest_a(0, 3)
    add_products(0, 3, 0, BS)
    pass_a(1, 2)
    pass_b(1, 2)
    pass_b(1, 3)
    rest_a(0, 2)
    add_products(0, 2, 0, BS)
    pass_a(1, 3)
    rest_b(1)
    add_products(1, 0, 0, BS)
    pass_a(1, 4)
    pass_a(1, 5)
    rest_a(1, 1)
    add_products(1, 1, 0, BS)
    rest_a(1, 3)
    add_products(1, 3, 0, BS)
    rest_a(1, 2)

    def start_of(r):
        return turned(y, r) * 32

    def end_products(r):
        add_products(1, 2, start_of(r), 32)
        for part in range(4):
            span = pl.ds(part * PART, PART)
            send(
                total.at[pl.ds(start_of(r) + (1 - core) * 16 + part * PART, PART)], other.at[r, span],
                twin_sem.at[0, r, part], twin_sem.at[1, r, part], twin,
            )

    def meet(r, part):
        landed(other.at[r, pl.ds(part * PART, PART)], twin_sem.at[1, r, part])

    def arrived(i):
        landed(q_in.at[i], q_recv.at[i])
        landed(s_in.at[i], s_recv.at[i])

    def chip_sum(r, slot):
        return total[start_of(r) + core * 16 + slot] + other[r, slot]

    def value(i, n):
        return q_in[i, n].astype(jnp.float32) * s_in[i, pl.ds(n, 1)]

    def tell(i, step, r, first, plus=None):
        meet(r, first // PART)

        def one(n, _):
            sums = chip_sum(r, first + n)
            if plus is not None:
                sums = sums + value(plus, n)
            top = jnp.maximum(jnp.max(jnp.abs(sums), axis=0, keepdims=True), TINY)
            q_out[i, n] = jnp.round(sums * (TOP / top)).astype(jnp.int32).astype(jnp.int16)
            s_out[i, pl.ds(n, 1)] = top * (1 / TOP)
            return 0

        lax.fori_loop(0, PART, one, 0)
        send(q_out.at[i], q_in.at[i], q_send.at[i], q_recv.at[i], y_to(step))
        send(s_out.at[i], s_in.at[i], s_send.at[i], s_recv.at[i], y_to(step))

    end_products(2)
    for part in range(2):
        tell(part, 1, 2, part * PART)
        tell(2 + part, -1, 2, (2 + part) * PART)
    end_products(1)
    end_products(3)
    for part in range(2):
        tell(4 + part, 1, 1, (2 + part) * PART)
    end_products(0)
    for part in range(2):
        tell(6 + part, -1, 3, part * PART)
    for part in range(2):
        arrived(part)
        tell(8 + part, 1, 1, part * PART, plus=part)
        arrived(2 + part)
        tell(10 + part, -1, 3, (2 + part) * PART, plus=2 + part)

    def finish(part, first, second):
        meet(0, part)
        arrived(first)
        arrived(second)

        def one(n, _):
            slot = part * PART + n
            sums = chip_sum(0, slot) + value(first, n) + value(second, n)
            done[slot] = sums.astype(jnp.bfloat16)
            return 0

        lax.fori_loop(0, PART, one, 0)
        span = pl.ds(part * PART, PART)
        hand_out_here(done.at[span], out_ref.at[span], out_sem.at[0, part], out_sem.at[1, part], owner)

    finish(0, 6, 8)
    finish(2, 4, 10)
    finish(1, 7, 9)
    finish(3, 5, 11)
    for part in range(4):
        landed(out_ref.at[pl.ds(part * PART, PART)], out_sem.at[1, part])
    for wait in waits:
        wait()


def per_device(a_blocks, a_rows, b_blocks, b_cols, c_pos):
    rows, cols = a_rows.transpose(1, 2, 3, 0), b_cols.transpose(1, 2, 3, 0)
    dma = pltpu.SemaphoreType.DMA
    vmem = pl.BlockSpec(memory_space=pltpu.VMEM)
    bf16, f32, i16, i32 = jnp.bfloat16, jnp.float32, jnp.int16, jnp.int32
    out = pl.pallas_call(
        kernel,
        out_shape=jax.ShapeDtypeStruct((16, BS, BS), bf16),
        in_specs=[ANY] * 5,
        out_specs=vmem,
        scratch_shapes=[
            *[pltpu.VMEM((ZERO + 1, BS, BS), bf16)] * 8,
            *[pltpu.VMEM((64, BS, BS), bf16)] * 2,
            pltpu.VMEM((2,) + c_pos.shape, i32),
            pltpu.VMEM((4, 16, 32), i32),
            pltpu.VMEM((4, 8, 32), i32),
            pltpu.VMEM((16, BS), i32),
            pltpu.SMEM((16, BS), i32),
            pltpu.VMEM((BS, BS, BS), f32),
            pltpu.VMEM((4, 16, BS, BS), f32),
            pltpu.VMEM((16, BS, BS), bf16),
            pltpu.VMEM((12, PART, BS, BS), i16),
            pltpu.VMEM((12, PART, BS), f32),
            pltpu.VMEM((12, PART, BS, BS), i16),
            pltpu.VMEM((12, PART, BS), f32),
            dma((2, 8)), dma((2, 8)), dma((2, 4, 6)), dma((2, 4, 6)),
            dma((2, 8)), dma((2, 8)), dma((2, 4, 4)), dma((2, 4, 4)), dma((5,)),
            dma((2, 4, 4)), dma((12,)), dma((12,)), dma((12,)), dma((12,)), dma((2, 4)),
        ],
        compiler_params=pltpu.CompilerParams(
            collective_id=0, has_side_effects=True, vmem_limit_bytes=60 * 2**20
        ),
        name="block_product",
    )(a_blocks.reshape(64, BS, BS), b_blocks.reshape(32, BS, BS), c_pos, rows, cols)
    return out[None, None]


def solution(mesh):
    placed = (
        P(None, "col", "row", "depth", None, None),
        P(),
        P(None, "row", "col", "depth", None, None),
        P(),
        P("row", "col", None),
    )
    return jax.shard_map(
        per_device,
        mesh=mesh,
        in_specs=placed,
        out_specs=P("row", "col", "depth", None, None),
        check_vma=False,
    )
```

```python
import jax
import jax.numpy as jnp
from jax import lax
from jax.experimental import pallas as pl
from jax.experimental.pallas import tpu as pltpu
from jax.sharding import PartitionSpec as P

MESH = pl.DeviceIdType.MESH
BS = 128
NBL = 16
ANY = pl.BlockSpec(memory_space=pl.ANY)


def place():
    row, z, depth = lax.axis_index("row"), lax.axis_index("col"), lax.axis_index("depth")
    return row // 2, depth % 2, row % 2, depth // 2, z


def device(x_hi, x_lo, core, y, z):
    return (x_hi * 2 + core, z, y * 2 + x_lo)


def remote(src, dst, send, recv, to):
    return pltpu.make_async_remote_copy(
        src_ref=src, dst_ref=dst, send_sem=send, recv_sem=recv, device_id=to, device_id_type=MESH
    )


STEPS = (0, 1, 3, 2)
UNITS = ((0, 0), (0, 1), (1, None), (2, None), (3, 0), (3, 1))
TOP = 32767.0
TINY = 2e-34
PART = 4
PARTS = 8 // PART
ZERO = 32
NONE = ZERO * 64


def kernel(
    a_ref, b_ref, c_ref, rows_ref, cols_ref, out_ref,
    a00, a01, a02, a03, a10, a11, a12, a13, b0, b1, spots, rows, cols, codes, jobs, total, other, done, q_out, s_out, q_in, s_in,
    az_out, az_recv, az_ring, az_got, bx_out, bx_recv, bx_ring, bx_got, c_sem,
    twin_sem, q_send, q_recv, s_send, s_recv, out_sem,
):
    x_hi, x_lo, core, y, z = place()
    x = x_hi * 2 + x_lo
    same = x_lo == core
    apart = jnp.where(same, 0, 1)
    a_half, b_half = ((a00, a01, a02, a03), (a10, a11, a12, a13)), (b0, b1)

    def turned(at, step):
        return lax.rem(at + step + 8, 4)

    def differ(at, flag):
        return at if flag == 0 else 1 - at

    def z_to(step):
        return device(x_hi, x_lo, core, y, turned(z, step))

    def x_to(step):
        to = turned(x, step)
        return device(to // 2, lax.rem(to, 2), core, y, z)

    def y_to(step):
        return device(x_hi, x_lo, core, turned(y, step), z)

    twin = device(x_hi, x_lo, 1 - core, y, z)
    owner = device(x_hi, core, x_lo, y, z)

    barrier = pltpu.get_barrier_semaphore()

    def greet(to):
        pl.semaphore_signal(barrier, inc=1, device_id=to, device_id_type=MESH)

    for dy in STEPS:
        for flag in range(2):
            if (dy, flag) == (0, 0):

                @pl.when(jnp.logical_not(same))
                def _():
                    greet(twin)

            else:
                greet(device(x_hi, differ(x_lo, flag), x_lo, turned(y, -dy), z))
                greet(device(x_hi, x_lo, differ(core, flag), turned(y, -dy), z))
    for step in (1, -1):
        greet(z_to(step))
        greet(x_to(step))
    pl.semaphore_wait(barrier, 18 + apart)

    waits = []

    def send(src, dst, sent, recv, to):
        copy = remote(src, dst, sent, recv, to)
        copy.start()
        waits.append(copy.wait_send)

    def settle(count):
        for _ in range(count):
            waits.pop(0)()

    def landed(piece, recv):
        remote(piece, piece, recv, recv, twin).wait_recv()

    def a_piece(half, back, at_y, at_lo):
        return a_half[half][back].at[pl.ds(at_y * 8 + at_lo * 4, 4)]

    def a_pieces(half, back, at_y):
        return a_half[half][back].at[pl.ds(at_y * 8, 8)]

    def b_piece(half, at_x, at_y, at_core):
        return b_half[half].at[pl.ds(at_x * 16 + at_y * 4 + at_core * 2, 2)]

    def b_pieces(half, at_x, at_y):
        return b_half[half].at[pl.ds(at_x * 16 + at_y * 4, 4)]

    def hand_out_a(half):
        for n, dy in enumerate(STEPS):
            for flag in range(2):
                to_y, to_core = turned(y, dy), differ(core, flag)
                group = (to_y * 2 + to_core) * 4 + half * 2
                src, dst = a_ref.at[pl.ds(group * 2, 4)], a_piece(half, 0, y, x_lo)
                sent, recv = az_out.at[half, n * 2 + flag], az_recv.at[half, n * 2 + apart]
                to = device(x_hi, core, to_core, to_y, z)
                if (dy, flag) == (0, 0):
                    hand_out_here(src, dst, sent, recv, to)
                else:
                    send(src, dst, sent, recv, to)

    def hand_out_b(half):
        for n, dy in enumerate(STEPS):
            for flag in range(2):
                to_y, to_core = turned(y, dy), differ(core, flag)
                group = (to_y * 2 + to_core) * 4 + half * 2
                src, dst = b_ref.at[pl.ds(group, 2)], b_piece(half, x, y, core)
                sent, recv = bx_out.at[half, n * 2 + flag], bx_recv.at[half, n * 2 + flag]
                if (dy, flag) == (0, 0):
                    pltpu.make_async_copy(src, dst, recv).start()
                else:
                    send(src, dst, sent, recv, device(x_hi, x_lo, to_core, to_y, z))

    def hand_out_here(src, dst, sent, recv, to):
        copy = remote(src, dst, sent, recv, to)
        stay = pltpu.make_async_copy(src, dst, recv)
        pl.when(same)(lambda: stay.start())
        pl.when(jnp.logical_not(same))(lambda: copy.start())
        waits.append(lambda: pl.when(jnp.logical_not(same))(lambda: copy.wait_send()))

    def a_unit(half, back, i):
        n, flag = UNITS[i]
        at = turned(y, -STEPS[n])
        return a_pieces(half, back, at) if flag is None else a_piece(half, back, at, differ(x_lo, flag))

    def turn_a(half, i):
        n, flag = UNITS[i]
        for one in range(2) if flag is None else (flag,):
            piece = a_piece(half, 0, turned(y, -STEPS[n]), differ(x_lo, one))
            landed(piece, az_recv.at[half, n * 2 + one])
        for back, step in ((1, 1), (3, -1)):
            send(
                a_unit(half, 0, i), a_unit(half, back, i), az_ring.at[half, back, i], az_got.at[half, back, i],
                z_to(step),
            )

    def pass_a(half, i):
        back, step = (1, 1) if i % 2 == 0 else (3, -1)
        landed(a_unit(half, back, i), az_got.at[half, back, i])
        send(
            a_unit(half, back, i), a_unit(half, 2, i), az_ring.at[half, 2, i], az_got.at[half, 2, i], z_to(step)
        )

    def rest_a(half, back):
        for i in range(len(UNITS)):
            if back == 2 or back != (1 if i % 2 == 0 else 3):
                landed(a_unit(half, back, i), az_got.at[half, back, i])

    def turn_b(half, n):
        at = turned(y, -STEPS[n])
        for flag in range(2):
            landed(b_piece(half, x, at, differ(core, flag)), bx_recv.at[half, n * 2 + flag])
        here = b_pieces(half, x, at)
        for back, step in ((1, 1), (3, -1)):
            send(here, here, bx_ring.at[half, back, n], bx_got.at[half, back, n], x_to(step))

    def pass_b(half, n):
        back, step = (1, 1) if n % 2 == 0 else (3, -1)
        there = b_pieces(half, turned(x, -back), turned(y, -STEPS[n]))
        landed(there, bx_got.at[half, back, n])
        send(there, there, bx_ring.at[half, 2, n], bx_got.at[half, 2, n], x_to(step))

    def rest_b(half):
        for n in range(4):
            for back in (3 if n % 2 == 0 else 1, 2):
                landed(b_pieces(half, turned(x, -back), turned(y, -STEPS[n])), bx_got.at[half, back, n])

    def pair_up():
        for copy in index_copies:
            copy.wait()
        landed(spots.at[1], c_sem.at[1])
        spot = jnp.where(same, spots[0, 0], spots[1, 0])
        kept_row = jnp.where(spot >= 0, spot // NBL, -2)
        kept_col = jnp.where(spot >= 0, spot % NBL, -2)

        def number_of(index, kept, number):
            slots, groups = index.shape

            def one(g):
                lane = lax.broadcasted_iota(jnp.int32, (slots, groups), 1)
                mine = jnp.sum(jnp.where(lane == g, index, 0), axis=1, keepdims=True)
                return jnp.max(jnp.where(mine == kept, number, -1), axis=0, keepdims=True)

            return one

        u = lax.broadcasted_iota(jnp.int32, (16, BS), 0)
        v = lax.broadcasted_iota(jnp.int32, (8, BS), 0)
        for m in range(4):
            row_of = number_of(rows[m], kept_row, (u >> 1) * 4 + (u & 1))
            col_of = number_of(cols[m], kept_col, (v & 1) * 16 + (v >> 1) * 4)
            for n in range(4):
                a_at, b_at = row_of((y * 2 + core) * 4 + n), col_of((y * 2 + core) * 4 + n)
                code = (a_at + n % 2 * 2) * 64 + b_at + (m // 2 * 32 + m % 2 * 2 + n % 2)
                codes[n * 4 + m : n * 4 + m + 1] = jnp.where((a_at >= 0) & (b_at >= 0), code, NONE)
        copy = pltpu.make_async_copy(codes, jobs, c_sem.at[2])
        copy.start()
        copy.wait()

    def add_products(half, back, first, count, fresh=False):
        left_ref, right_ref = a_half[half][back], b_half[half]
        k = half * 8 + turned(z, -back)

        def some(n, _):
            for s in range(32):
                slot = first + n * 32 + s
                one, two = jobs[k, slot], jobs[k + 4, slot]
                left = jnp.concatenate([left_ref[one >> 6], left_ref[two >> 6]], axis=1)
                right = jnp.concatenate([right_ref[one & 63], right_ref[two & 63]], axis=0)
                term = jnp.dot(left, right, preferred_element_type=jnp.float32)
                if fresh:
                    total[slot] = term
                else:
                    total[slot] += term
            return 0

        lax.fori_loop(0, count // 32, some, 0)

    hand_out_a(0)
    turn_a(0, 0)
    hand_out_b(0)
    send(c_ref, spots.at[1], c_sem.at[0], c_sem.at[1], twin)
    index_copies = [
        pltpu.make_async_copy(c_ref, spots.at[0], c_sem.at[2]),
        pltpu.make_async_copy(rows_ref.at[:, x], rows, c_sem.at[3]),
        pltpu.make_async_copy(cols_ref.at[:, z], cols, c_sem.at[4]),
    ]
    for copy in index_copies:
        copy.start()
    for half in a_half:
        for ref in half:
            ref[ZERO] = jnp.zeros((BS, BS), jnp.bfloat16)
    turn_a(0, 1)
    turn_b(0, 0)
    turn_a(0, 2)
    pass_a(0, 0)
    pass_a(0, 1)
    turn_a(0, 3)
    pass_a(0, 2)
    turn_a(0, 4)
    turn_a(0, 5)
    turn_b(0, 1)
    turn_b(0, 2)
    hand_out_a(1)
    hand_out_b(1)
    turn_b(0, 3)
    pass_a(0, 3)
    pass_b(0, 0)
    pass_b(0, 1)
    pass_a(0, 4)
    pass_a(0, 5)
    pass_b(0, 2)
    pass_b(0, 3)
    pair_up()
    turn_a(1, 0)
    turn_a(1, 1)
    turn_a(1, 2)
    turn_a(1, 3)
    turn_a(1, 4)
    turn_a(1, 5)
    turn_b(1, 0)
    turn_b(1, 1)
    rest_b(0)
    add_products(0, 0, 0, BS, fresh=True)
    turn_b(1, 2)
    turn_b(1, 3)
    rest_a(0, 1)
    add_products(0, 1, 0, BS)
    pass_a(1, 0)
    pass_a(1, 1)
    pass_b(1, 0)
    pass_b(1, 1)
    rest_a(0, 3)
    add_products(0, 3, 0, BS)
    pass_a(1, 2)
    pass_b(1, 2)
    pass_b(1, 3)
    rest_a(0, 2)
    add_products(0, 2, 0, BS)
    pass_a(1, 3)
    rest_b(1)
    add_products(1, 0, 0, BS)
    pass_a(1, 4)
    pass_a(1, 5)
    rest_a(1, 1)
    add_products(1, 1, 0, BS)
    rest_a(1, 3)
    add_products(1, 3, 0, BS)
    rest_a(1, 2)

    def start_of(r):
        return turned(y, r) * 32

    def end_products(r):
        add_products(1, 2, start_of(r), 32)
        for part in range(4):
            span = pl.ds(part * PART, PART)
            send(
                total.at[pl.ds(start_of(r) + (1 - core) * 16 + part * PART, PART)], other.at[r, span],
                twin_sem.at[0, r, part], twin_sem.at[1, r, part], twin,
            )

    def meet(r, part):
        landed(other.at[r, pl.ds(part * PART, PART)], twin_sem.at[1, r, part])

    def arrived(i):
        landed(q_in.at[i], q_recv.at[i])
        landed(s_in.at[i], s_recv.at[i])

    def chip_sum(r, slot):
        return total[start_of(r) + core * 16 + slot] + other[r, slot]

    def value(i, n):
        return q_in[i, n].astype(jnp.float32) * s_in[i, pl.ds(n, 1)]

    def tell(i, step, r, first, plus=None):
        meet(r, first // PART)

        def term(n):
            sums = chip_sum(r, first + n)
            return sums if plus is None else sums + value(plus, n)

        tops = [
            jnp.maximum(jnp.max(jnp.abs(term(n)), axis=0, keepdims=True), TINY) for n in range(PART)
        ]
        for n, top in enumerate(tops):
            s_out[i, n : n + 1] = top * (1 / TOP)
        scales = [TOP / top for top in tops]
        for n, scale in enumerate(scales):
            q_out[i, n] = jnp.round(term(n) * scale).astype(jnp.int32).astype(jnp.int16)
        send(q_out.at[i], q_in.at[i], q_send.at[i], q_recv.at[i], y_to(step))
        send(s_out.at[i], s_in.at[i], s_send.at[i], s_recv.at[i], y_to(step))

    gathered = len(waits)
    end_products(2)
    for part in range(PARTS):
        tell(part, 1, 2, part * PART)
        tell(PARTS + part, -1, 2, 8 + part * PART)
    end_products(1)
    for part in range(PARTS):
        tell(2 * PARTS + part, 1, 1, 8 + part * PART)
    end_products(3)
    for part in range(PARTS // 2):
        tell(3 * PARTS + part, -1, 3, part * PART)
    end_products(0)
    settle(gathered)
    handed = len(waits)
    for part in range(PARTS):
        arrived(PARTS + part)
        tell(5 * PARTS + part, -1, 3, 8 + part * PART, plus=PARTS + part)
        arrived(part)
        tell(4 * PARTS + part, 1, 1, part * PART, plus=part)
    for part in range(PARTS // 2, PARTS):
        tell(3 * PARTS + part, -1, 3, part * PART)

    def finish(part, first, second):
        meet(0, part)
        arrived(first)
        arrived(second)

        def one(n, _):
            slot = part * PART + n
            sums = chip_sum(0, slot) + value(first, n) + value(second, n)
            done[slot] = sums.astype(jnp.bfloat16)
            return 0

        lax.fori_loop(0, PART, one, 0)
        span = pl.ds(part * PART, PART)
        hand_out_here(done.at[span], out_ref.at[span], out_sem.at[0, part], out_sem.at[1, part], owner)

    settle(handed)
    for part in range(PARTS):
        finish(PARTS + part, 2 * PARTS + part, 5 * PARTS + part)
        finish(part, 3 * PARTS + part, 4 * PARTS + part)
    for part in range(2 * PARTS):
        landed(out_ref.at[pl.ds(part * PART, PART)], out_sem.at[1, part])
    settle(len(waits))


def per_device(a_blocks, a_rows, b_blocks, b_cols, c_pos):
    rows, cols = a_rows.transpose(1, 2, 3, 0), b_cols.transpose(1, 2, 3, 0)
    dma = pltpu.SemaphoreType.DMA
    vmem = pl.BlockSpec(memory_space=pltpu.VMEM)
    bf16, f32, i16, i32 = jnp.bfloat16, jnp.float32, jnp.int16, jnp.int32
    out = pl.pallas_call(
        kernel,
        out_shape=jax.ShapeDtypeStruct((16, BS, BS), bf16),
        in_specs=[pl.BlockSpec(memory_space=pltpu.HBM)] * 5,
        out_specs=vmem,
        scratch_shapes=[
            *[pltpu.VMEM((ZERO + 1, BS, BS), bf16)] * 8,
            *[pltpu.VMEM((64, BS, BS), bf16)] * 2,
            pltpu.VMEM((2,) + c_pos.shape, i32),
            pltpu.VMEM((4, 16, 32), i32),
            pltpu.VMEM((4, 8, 32), i32),
            pltpu.VMEM((16, BS), i32),
            pltpu.SMEM((16, BS), i32),
            pltpu.VMEM((BS, BS, BS), f32),
            pltpu.VMEM((4, 16, BS, BS), f32),
            pltpu.VMEM((16, BS, BS), bf16),
            pltpu.VMEM((6 * PARTS, PART, BS, BS), i16),
            pltpu.VMEM((6 * PARTS, PART, BS), f32),
            pltpu.VMEM((6 * PARTS, PART, BS, BS), i16),
            pltpu.VMEM((6 * PARTS, PART, BS), f32),
            dma((2, 8)), dma((2, 8)), dma((2, 4, 6)), dma((2, 4, 6)),
            dma((2, 8)), dma((2, 8)), dma((2, 4, 4)), dma((2, 4, 4)), dma((5,)),
            dma((2, 4, 2 * PARTS)), *[dma((6 * PARTS,))] * 4, dma((2, 2 * PARTS)),
        ],
        compiler_params=pltpu.CompilerParams(
            collective_id=0, has_side_effects=True, vmem_limit_bytes=44 * 2**20
        ),
        name="block_product",
    )(*(pltpu.with_memory_space_constraint(x, pltpu.HBM) for x in (a_blocks.reshape(64, BS, BS), b_blocks.reshape(32, BS, BS), c_pos, rows, cols)))
    return out[None, None]


def solution(mesh):
    placed = (
        P(None, "col", "row", "depth", None, None),
        P(),
        P(None, "row", "col", "depth", None, None),
        P(),
        P("row", "col", None),
    )
    return jax.shard_map(
        per_device,
        mesh=mesh,
        in_specs=placed,
        out_specs=P("row", "col", "depth", None, None),
        check_vma=False,
    )
```

```python
import jax
import jax.numpy as jnp
from jax import lax
from jax.experimental import pallas as pl
from jax.experimental.pallas import tpu as pltpu
from jax.sharding import PartitionSpec as P

MESH = pl.DeviceIdType.MESH
BS = 128
NBL = 16
ANY = pl.BlockSpec(memory_space=pl.ANY)


def place():
    row, z, depth = lax.axis_index("row"), lax.axis_index("col"), lax.axis_index("depth")
    return row // 2, depth % 2, row % 2, depth // 2, z


def device(x_hi, x_lo, core, y, z):
    return (x_hi * 2 + core, z, y * 2 + x_lo)


def remote(src, dst, send, recv, to):
    return pltpu.make_async_remote_copy(
        src_ref=src, dst_ref=dst, send_sem=send, recv_sem=recv, device_id=to, device_id_type=MESH
    )


STEPS = (0, 1, 3, 2)
UNITS = ((0, 0), (0, 1), (1, None), (2, None), (3, 0), (3, 1))
TOP = 32767.0
TINY = 2e-34
PART = 4
PARTS = 8 // PART
ZERO = 32
NONE = ZERO * 64


def kernel(
    a_ref, b_ref, c_ref, rows_ref, cols_ref, out_ref,
    a00, a01, a02, a03, a10, a11, a12, a13, b0, b1, spots, rows, cols, codes, jobs, total, other, done, q_out, s_out, q_in, s_in,
    az_out, az_recv, az_ring, az_got, bx_out, bx_recv, bx_ring, bx_got, c_sem,
    twin_sem, q_send, q_recv, s_send, s_recv, out_sem,
):
    x_hi, x_lo, core, y, z = place()
    x = x_hi * 2 + x_lo
    same = x_lo == core
    apart = jnp.where(same, 0, 1)
    a_half, b_half = ((a00, a01, a02, a03), (a10, a11, a12, a13)), (b0, b1)

    def turned(at, step):
        return lax.rem(at + step + 8, 4)

    def differ(at, flag):
        return at if flag == 0 else 1 - at

    def z_to(step):
        return device(x_hi, x_lo, core, y, turned(z, step))

    def x_to(step):
        to = turned(x, step)
        return device(to // 2, lax.rem(to, 2), core, y, z)

    def y_to(step):
        return device(x_hi, x_lo, core, turned(y, step), z)

    twin = device(x_hi, x_lo, 1 - core, y, z)
    owner = device(x_hi, core, x_lo, y, z)

    barrier = pltpu.get_barrier_semaphore()

    def greet(to):
        pl.semaphore_signal(barrier, inc=1, device_id=to, device_id_type=MESH)

    for dy in STEPS:
        for flag in range(2):
            if (dy, flag) == (0, 0):

                @pl.when(jnp.logical_not(same))
                def _():
                    greet(twin)

            else:
                greet(device(x_hi, differ(x_lo, flag), x_lo, turned(y, -dy), z))
                greet(device(x_hi, x_lo, differ(core, flag), turned(y, -dy), z))
    for step in (1, -1):
        greet(z_to(step))
        greet(x_to(step))
    index_copies = [
        pltpu.make_async_copy(c_ref, spots.at[0], c_sem.at[2]),
        pltpu.make_async_copy(rows_ref.at[:, x], rows, c_sem.at[3]),
        pltpu.make_async_copy(cols_ref.at[:, z], cols, c_sem.at[4]),
    ]
    for copy in index_copies:
        copy.start()
    for half in a_half:
        for ref in half:
            ref[ZERO] = jnp.zeros((BS, BS), jnp.bfloat16)
    pl.semaphore_wait(barrier, 18 + apart)

    waits = []

    def send(src, dst, sent, recv, to):
        copy = remote(src, dst, sent, recv, to)
        copy.start()
        waits.append(copy.wait_send)

    def settle(count):
        for _ in range(count):
            waits.pop(0)()

    def landed(piece, recv):
        remote(piece, piece, recv, recv, twin).wait_recv()

    def a_piece(half, back, at_y, at_lo):
        return a_half[half][back].at[pl.ds(at_y * 8 + at_lo * 4, 4)]

    def a_pieces(half, back, at_y):
        return a_half[half][back].at[pl.ds(at_y * 8, 8)]

    def b_piece(half, at_x, at_y, at_core):
        return b_half[half].at[pl.ds(at_x * 16 + at_y * 4 + at_core * 2, 2)]

    def b_pieces(half, at_x, at_y):
        return b_half[half].at[pl.ds(at_x * 16 + at_y * 4, 4)]

    def hand_out_a(half):
        for n, dy in enumerate(STEPS):
            for flag in range(2):
                to_y, to_core = turned(y, dy), differ(core, flag)
                group = (to_y * 2 + to_core) * 4 + half * 2
                src, dst = a_ref.at[pl.ds(group * 2, 4)], a_piece(half, 0, y, x_lo)
                sent, recv = az_out.at[half, n * 2 + flag], az_recv.at[half, n * 2 + apart]
                to = device(x_hi, core, to_core, to_y, z)
                if (dy, flag) == (0, 0):
                    hand_out_here(src, dst, sent, recv, to)
                else:
                    send(src, dst, sent, recv, to)

    def hand_out_b(half):
        for n, dy in enumerate(STEPS):
            for flag in range(2):
                to_y, to_core = turned(y, dy), differ(core, flag)
                group = (to_y * 2 + to_core) * 4 + half * 2
                src, dst = b_ref.at[pl.ds(group, 2)], b_piece(half, x, y, core)
                sent, recv = bx_out.at[half, n * 2 + flag], bx_recv.at[half, n * 2 + flag]
                if (dy, flag) == (0, 0):
                    pltpu.make_async_copy(src, dst, recv).start()
                else:
                    send(src, dst, sent, recv, device(x_hi, x_lo, to_core, to_y, z))

    def hand_out_here(src, dst, sent, recv, to):
        copy = remote(src, dst, sent, recv, to)
        stay = pltpu.make_async_copy(src, dst, recv)
        pl.when(same)(lambda: stay.start())
        pl.when(jnp.logical_not(same))(lambda: copy.start())
        waits.append(lambda: pl.when(jnp.logical_not(same))(lambda: copy.wait_send()))

    def a_unit(half, back, i):
        n, flag = UNITS[i]
        at = turned(y, -STEPS[n])
        return a_pieces(half, back, at) if flag is None else a_piece(half, back, at, differ(x_lo, flag))

    def turn_a(half, i):
        n, flag = UNITS[i]
        for one in range(2) if flag is None else (flag,):
            piece = a_piece(half, 0, turned(y, -STEPS[n]), differ(x_lo, one))
            landed(piece, az_recv.at[half, n * 2 + one])
        for back, step in ((1, 1), (3, -1)):
            send(
                a_unit(half, 0, i), a_unit(half, back, i), az_ring.at[half, back, i], az_got.at[half, back, i],
                z_to(step),
            )

    def pass_a(half, i):
        back, step = (1, 1) if i % 2 == 0 else (3, -1)
        landed(a_unit(half, back, i), az_got.at[half, back, i])
        send(
            a_unit(half, back, i), a_unit(half, 2, i), az_ring.at[half, 2, i], az_got.at[half, 2, i], z_to(step)
        )

    def rest_a(half, back):
        for i in range(len(UNITS)):
            if back == 2 or back != (1 if i % 2 == 0 else 3):
                landed(a_unit(half, back, i), az_got.at[half, back, i])

    def turn_b(half, n):
        at = turned(y, -STEPS[n])
        for flag in range(2):
            landed(b_piece(half, x, at, differ(core, flag)), bx_recv.at[half, n * 2 + flag])
        here = b_pieces(half, x, at)
        for back, step in ((1, 1), (3, -1)):
            send(here, here, bx_ring.at[half, back, n], bx_got.at[half, back, n], x_to(step))

    def pass_b(half, n):
        back, step = (1, 1) if n % 2 == 0 else (3, -1)
        there = b_pieces(half, turned(x, -back), turned(y, -STEPS[n]))
        landed(there, bx_got.at[half, back, n])
        send(there, there, bx_ring.at[half, 2, n], bx_got.at[half, 2, n], x_to(step))

    def rest_b(half):
        for n in range(4):
            for back in (3 if n % 2 == 0 else 1, 2):
                landed(b_pieces(half, turned(x, -back), turned(y, -STEPS[n])), bx_got.at[half, back, n])

    def pair_up():
        for copy in index_copies:
            copy.wait()
        landed(spots.at[1], c_sem.at[1])
        spot = jnp.where(same, spots[0, 0], spots[1, 0])
        kept_row = jnp.where(spot >= 0, spot // NBL, -2)
        kept_col = jnp.where(spot >= 0, spot % NBL, -2)

        def number_of(index, kept, number):
            slots, groups = index.shape

            def one(g):
                lane = lax.broadcasted_iota(jnp.int32, (slots, groups), 1)
                mine = jnp.sum(jnp.where(lane == g, index, 0), axis=1, keepdims=True)
                return jnp.max(jnp.where(mine == kept, number, -1), axis=0, keepdims=True)

            return one

        u = lax.broadcasted_iota(jnp.int32, (16, BS), 0)
        v = lax.broadcasted_iota(jnp.int32, (8, BS), 0)
        for m in range(4):
            row_of = number_of(rows[m], kept_row, (u >> 1) * 4 + (u & 1))
            col_of = number_of(cols[m], kept_col, (v & 1) * 16 + (v >> 1) * 4)
            for n in range(4):
                a_at, b_at = row_of((y * 2 + core) * 4 + n), col_of((y * 2 + core) * 4 + n)
                code = (a_at + n % 2 * 2) * 64 + b_at + (m // 2 * 32 + m % 2 * 2 + n % 2)
                codes[n * 4 + m : n * 4 + m + 1] = jnp.where((a_at >= 0) & (b_at >= 0), code, NONE)
        copy = pltpu.make_async_copy(codes, jobs, c_sem.at[2])
        copy.start()
        copy.wait()

    def add_products(half, back, first, count, fresh=False, width=32):
        left_ref, right_ref = a_half[half][back], b_half[half]
        k = half * 8 + turned(z, -back)

        def some(n, _):
            for s in range(width):
                slot = first + n * width + s
                one, two = jobs[k, slot], jobs[k + 4, slot]
                left = jnp.concatenate([left_ref[one >> 6], left_ref[two >> 6]], axis=1)
                right = jnp.concatenate([right_ref[one & 63], right_ref[two & 63]], axis=0)
                term = jnp.dot(left, right, preferred_element_type=jnp.float32)
                if fresh:
                    total[slot] = term
                else:
                    total[slot] += term
            return 0

        lax.fori_loop(0, count // width, some, 0)

    hand_out_a(0)
    turn_a(0, 0)
    hand_out_b(0)
    send(c_ref, spots.at[1], c_sem.at[0], c_sem.at[1], twin)
    turn_a(0, 1)
    turn_b(0, 0)
    turn_a(0, 2)
    pass_a(0, 0)
    pass_a(0, 1)
    turn_a(0, 3)
    pass_a(0, 2)
    turn_a(0, 4)
    turn_a(0, 5)
    turn_b(0, 1)
    turn_b(0, 2)
    hand_out_a(1)
    hand_out_b(1)
    turn_b(0, 3)
    pass_a(0, 3)
    pass_b(0, 0)
    pass_b(0, 1)
    pass_a(0, 4)
    pass_a(0, 5)
    pass_b(0, 2)
    pass_b(0, 3)
    pair_up()
    turn_a(1, 0)
    turn_a(1, 1)
    turn_a(1, 2)
    turn_a(1, 3)
    turn_a(1, 4)
    turn_a(1, 5)
    turn_b(1, 0)
    turn_b(1, 1)
    rest_b(0)
    add_products(0, 0, 0, BS, fresh=True)
    turn_b(1, 2)
    turn_b(1, 3)
    rest_a(0, 1)
    add_products(0, 1, 0, BS)
    pass_a(1, 0)
    pass_a(1, 1)
    pass_b(1, 0)
    pass_b(1, 1)
    rest_a(0, 3)
    add_products(0, 3, 0, BS)
    pass_a(1, 2)
    pass_b(1, 2)
    pass_b(1, 3)
    rest_a(0, 2)
    add_products(0, 2, 0, BS)
    pass_a(1, 3)
    rest_b(1)
    add_products(1, 0, 0, BS)
    pass_a(1, 4)
    pass_a(1, 5)
    rest_a(1, 1)
    add_products(1, 1, 0, BS)
    rest_a(1, 3)
    add_products(1, 3, 0, BS)
    rest_a(1, 2)

    def start_of(r):
        return turned(y, r) * 32

    def end_products(r):
        add_products(1, 2, start_of(r) + (1 - core) * 16, 16, width=16)
        for part in range(4):
            span = pl.ds(part * PART, PART)
            send(
                total.at[pl.ds(start_of(r) + (1 - core) * 16 + part * PART, PART)], other.at[r, span],
                twin_sem.at[0, r, part], twin_sem.at[1, r, part], twin,
            )
        add_products(1, 2, start_of(r) + core * 16, 16, width=16)

    def meet(r, part):
        landed(other.at[r, pl.ds(part * PART, PART)], twin_sem.at[1, r, part])

    def arrived(i):
        landed(q_in.at[i], q_recv.at[i])
        landed(s_in.at[i], s_recv.at[i])

    def chip_sum(r, slot):
        return total[start_of(r) + core * 16 + slot] + other[r, slot]

    def value(i, n):
        return q_in[i, n].astype(jnp.float32) * s_in[i, pl.ds(n, 1)]

    def tell(i, step, r, first, plus=None):
        meet(r, first // PART)

        def term(n):
            sums = chip_sum(r, first + n)
            return sums if plus is None else sums + value(plus, n)

        tops = [
            jnp.maximum(jnp.max(jnp.abs(term(n)), axis=0, keepdims=True), TINY) for n in range(PART)
        ]
        for n, top in enumerate(tops):
            s_out[i, n : n + 1] = top * (1 / TOP)
        scales = [TOP / top for top in tops]
        for n, scale in enumerate(scales):
            q_out[i, n] = jnp.round(term(n) * scale).astype(jnp.int32).astype(jnp.int16)
        send(q_out.at[i], q_in.at[i], q_send.at[i], q_recv.at[i], y_to(step))
        send(s_out.at[i], s_in.at[i], s_send.at[i], s_recv.at[i], y_to(step))

    gathered = len(waits)
    end_products(2)
    for part in range(PARTS):
        tell(part, 1, 2, part * PART)
        tell(PARTS + part, -1, 2, 8 + part * PART)
    end_products(1)
    for part in range(PARTS):
        tell(2 * PARTS + part, 1, 1, 8 + part * PART)
    end_products(3)
    for part in range(PARTS // 2):
        tell(3 * PARTS + part, -1, 3, part * PART)
    end_products(0)
    settle(gathered)
    handed = len(waits)
    for part in range(PARTS):
        arrived(PARTS + part)
        tell(5 * PARTS + part, -1, 3, 8 + part * PART, plus=PARTS + part)
        arrived(part)
        tell(4 * PARTS + part, 1, 1, part * PART, plus=part)
    for part in range(PARTS // 2, PARTS):
        tell(3 * PARTS + part, -1, 3, part * PART)

    def finish(part, first, second):
        meet(0, part)
        arrived(first)
        arrived(second)

        def one(n, _):
            slot = part * PART + n
            sums = chip_sum(0, slot) + value(first, n) + value(second, n)
            done[slot] = sums.astype(jnp.bfloat16)
            return 0

        lax.fori_loop(0, PART, one, 0)
        span = pl.ds(part * PART, PART)
        hand_out_here(done.at[span], out_ref.at[span], out_sem.at[0, part], out_sem.at[1, part], owner)

    settle(handed)
    for part in range(PARTS):
        finish(PARTS + part, 2 * PARTS + part, 5 * PARTS + part)
        finish(part, 3 * PARTS + part, 4 * PARTS + part)
    for part in range(2 * PARTS):
        landed(out_ref.at[pl.ds(part * PART, PART)], out_sem.at[1, part])
    settle(len(waits))


def per_device(a_blocks, a_rows, b_blocks, b_cols, c_pos):
    rows, cols = a_rows.transpose(1, 2, 3, 0), b_cols.transpose(1, 2, 3, 0)
    dma = pltpu.SemaphoreType.DMA
    vmem = pl.BlockSpec(memory_space=pltpu.VMEM)
    bf16, f32, i16, i32 = jnp.bfloat16, jnp.float32, jnp.int16, jnp.int32
    out = pl.pallas_call(
        kernel,
        out_shape=jax.ShapeDtypeStruct((16, BS, BS), bf16),
        in_specs=[pl.BlockSpec(memory_space=pltpu.HBM)] * 5,
        out_specs=vmem,
        scratch_shapes=[
            *[pltpu.VMEM((ZERO + 1, BS, BS), bf16)] * 8,
            *[pltpu.VMEM((64, BS, BS), bf16)] * 2,
            pltpu.VMEM((2,) + c_pos.shape, i32),
            pltpu.VMEM((4, 16, 32), i32),
            pltpu.VMEM((4, 8, 32), i32),
            pltpu.VMEM((16, BS), i32),
            pltpu.SMEM((16, BS), i32),
            pltpu.VMEM((BS, BS, BS), f32),
            pltpu.VMEM((4, 16, BS, BS), f32),
            pltpu.VMEM((16, BS, BS), bf16),
            pltpu.VMEM((6 * PARTS, PART, BS, BS), i16),
            pltpu.VMEM((6 * PARTS, PART, BS), f32),
            pltpu.VMEM((6 * PARTS, PART, BS, BS), i16),
            pltpu.VMEM((6 * PARTS, PART, BS), f32),
            dma((2, 8)), dma((2, 8)), dma((2, 4, 6)), dma((2, 4, 6)),
            dma((2, 8)), dma((2, 8)), dma((2, 4, 4)), dma((2, 4, 4)), dma((5,)),
            dma((2, 4, 2 * PARTS)), *[dma((6 * PARTS,))] * 4, dma((2, 2 * PARTS)),
        ],
        compiler_params=pltpu.CompilerParams(
            collective_id=0, has_side_effects=True, vmem_limit_bytes=44 * 2**20
        ),
        name="block_product",
    )(*(pltpu.with_memory_space_constraint(x, pltpu.HBM) for x in (a_blocks.reshape(64, BS, BS), b_blocks.reshape(32, BS, BS), c_pos, rows, cols)))
    return out[None, None]


def solution(mesh):
    placed = (
        P(None, "col", "row", "depth", None, None),
        P(),
        P(None, "row", "col", "depth", None, None),
        P(),
        P("row", "col", None),
    )
    return jax.shard_map(
        per_device,
        mesh=mesh,
        in_specs=placed,
        out_specs=P("row", "col", "depth", None, None),
        check_vma=False,
    )
```

```python
import jax
import jax.numpy as jnp
from jax import lax
from jax.experimental import pallas as pl
from jax.experimental.pallas import tpu as pltpu
from jax.sharding import PartitionSpec as P

MESH = pl.DeviceIdType.MESH
BS = 128
NBL = 16
ANY = pl.BlockSpec(memory_space=pl.ANY)


def place():
    row, z, depth = lax.axis_index("row"), lax.axis_index("col"), lax.axis_index("depth")
    return row // 2, depth % 2, row % 2, depth // 2, z


def device(x_hi, x_lo, core, y, z):
    return (x_hi * 2 + core, z, y * 2 + x_lo)


def remote(src, dst, send, recv, to):
    return pltpu.make_async_remote_copy(
        src_ref=src, dst_ref=dst, send_sem=send, recv_sem=recv, device_id=to, device_id_type=MESH
    )


STEPS = (0, 1, 3, 2)
UNITS = ((0, 0), (0, 1), (1, None), (2, None), (3, 0), (3, 1))
TOP = 32767.0
TINY = 2e-34
PART = 4
PARTS = 8 // PART
ZERO = 32
NONE = ZERO * 64


def kernel(
    a_ref, b_ref, c_ref, rows_ref, cols_ref, out_ref,
    a00, a01, a02, a03, a10, a11, a12, a13, b0, b1, spots, rows, cols, codes, jobs, total, other, done, q_out, s_out, q_in, s_in,
    az_out, az_recv, az_ring, az_got, bx_out, bx_recv, bx_ring, bx_got, c_sem,
    twin_sem, q_send, q_recv, s_send, s_recv, out_sem,
):
    x_hi, x_lo, core, y, z = place()
    x = x_hi * 2 + x_lo
    same = x_lo == core
    apart = jnp.where(same, 0, 1)
    a_half, b_half = ((a00, a01, a02, a03), (a10, a11, a12, a13)), (b0, b1)

    def turned(at, step):
        return lax.rem(at + step + 8, 4)

    def differ(at, flag):
        return at if flag == 0 else 1 - at

    def z_to(step):
        return device(x_hi, x_lo, core, y, turned(z, step))

    def x_to(step):
        to = turned(x, step)
        return device(to // 2, lax.rem(to, 2), core, y, z)

    def y_to(step):
        return device(x_hi, x_lo, core, turned(y, step), z)

    twin = device(x_hi, x_lo, 1 - core, y, z)
    owner = device(x_hi, core, x_lo, y, z)

    barrier = pltpu.get_barrier_semaphore()

    def greet(to):
        pl.semaphore_signal(barrier, inc=1, device_id=to, device_id_type=MESH)

    for dy in STEPS:
        for flag in range(2):
            if (dy, flag) == (0, 0):

                @pl.when(jnp.logical_not(same))
                def _():
                    greet(twin)

            else:
                greet(device(x_hi, differ(x_lo, flag), x_lo, turned(y, -dy), z))
                greet(device(x_hi, x_lo, differ(core, flag), turned(y, -dy), z))
    for step in (1, -1):
        greet(z_to(step))
        greet(x_to(step))
    index_copies = [
        pltpu.make_async_copy(c_ref, spots.at[0], c_sem.at[2]),
        pltpu.make_async_copy(rows_ref.at[:, x], rows, c_sem.at[3]),
        pltpu.make_async_copy(cols_ref.at[:, z], cols, c_sem.at[4]),
    ]
    for copy in index_copies:
        copy.start()
    for half in a_half:
        for ref in half:
            ref[ZERO] = jnp.zeros((BS, BS), jnp.bfloat16)
    pl.semaphore_wait(barrier, 18 + apart)

    waits = []

    def send(src, dst, sent, recv, to):
        copy = remote(src, dst, sent, recv, to)
        copy.start()
        waits.append(copy.wait_send)

    def settle(count):
        for _ in range(count):
            waits.pop(0)()

    def landed(piece, recv):
        remote(piece, piece, recv, recv, twin).wait_recv()

    def a_piece(half, back, at_y, at_lo):
        return a_half[half][back].at[pl.ds(at_y * 8 + at_lo * 4, 4)]

    def a_pieces(half, back, at_y):
        return a_half[half][back].at[pl.ds(at_y * 8, 8)]

    def b_piece(half, at_x, at_y, at_core):
        return b_half[half].at[pl.ds(at_x * 16 + at_y * 4 + at_core * 2, 2)]

    def b_pieces(half, at_x, at_y):
        return b_half[half].at[pl.ds(at_x * 16 + at_y * 4, 4)]

    def hand_out_a(half):
        for n, dy in enumerate(STEPS):
            for flag in range(2):
                to_y, to_core = turned(y, dy), differ(core, flag)
                group = (to_y * 2 + to_core) * 4 + half * 2
                src, dst = a_ref.at[pl.ds(group * 2, 4)], a_piece(half, 0, y, x_lo)
                sent, recv = az_out.at[half, n * 2 + flag], az_recv.at[half, n * 2 + apart]
                to = device(x_hi, core, to_core, to_y, z)
                if (dy, flag) == (0, 0):
                    hand_out_here(src, dst, sent, recv, to)
                else:
                    send(src, dst, sent, recv, to)

    def hand_out_b(half):
        for n, dy in enumerate(STEPS):
            for flag in range(2):
                to_y, to_core = turned(y, dy), differ(core, flag)
                group = (to_y * 2 + to_core) * 4 + half * 2
                src, dst = b_ref.at[pl.ds(group, 2)], b_piece(half, x, y, core)
                sent, recv = bx_out.at[half, n * 2 + flag], bx_recv.at[half, n * 2 + flag]
                if (dy, flag) == (0, 0):
                    pltpu.make_async_copy(src, dst, recv).start()
                else:
                    send(src, dst, sent, recv, device(x_hi, x_lo, to_core, to_y, z))

    def hand_out_here(src, dst, sent, recv, to):
        copy = remote(src, dst, sent, recv, to)
        stay = pltpu.make_async_copy(src, dst, recv)
        pl.when(same)(lambda: stay.start())
        pl.when(jnp.logical_not(same))(lambda: copy.start())
        waits.append(lambda: pl.when(jnp.logical_not(same))(lambda: copy.wait_send()))

    def a_unit(half, back, i):
        n, flag = UNITS[i]
        at = turned(y, -STEPS[n])
        return a_pieces(half, back, at) if flag is None else a_piece(half, back, at, differ(x_lo, flag))

    def turn_a(half, i):
        n, flag = UNITS[i]
        for one in range(2) if flag is None else (flag,):
            piece = a_piece(half, 0, turned(y, -STEPS[n]), differ(x_lo, one))
            landed(piece, az_recv.at[half, n * 2 + one])
        for back, step in ((1, 1), (3, -1)):
            send(
                a_unit(half, 0, i), a_unit(half, back, i), az_ring.at[half, back, i], az_got.at[half, back, i],
                z_to(step),
            )

    def pass_a(half, i):
        back, step = (1, 1) if i % 2 == 0 else (3, -1)
        landed(a_unit(half, back, i), az_got.at[half, back, i])
        send(
            a_unit(half, back, i), a_unit(half, 2, i), az_ring.at[half, 2, i], az_got.at[half, 2, i], z_to(step)
        )

    def rest_a(half, back):
        for i in range(len(UNITS)):
            if back == 2 or back != (1 if i % 2 == 0 else 3):
                landed(a_unit(half, back, i), az_got.at[half, back, i])

    def turn_b(half, n):
        at = turned(y, -STEPS[n])
        for flag in range(2):
            landed(b_piece(half, x, at, differ(core, flag)), bx_recv.at[half, n * 2 + flag])
        here = b_pieces(half, x, at)
        for back, step in ((1, 1), (3, -1)):
            send(here, here, bx_ring.at[half, back, n], bx_got.at[half, back, n], x_to(step))

    def pass_b(half, n):
        back, step = (1, 1) if n % 2 == 0 else (3, -1)
        there = b_pieces(half, turned(x, -back), turned(y, -STEPS[n]))
        landed(there, bx_got.at[half, back, n])
        send(there, there, bx_ring.at[half, 2, n], bx_got.at[half, 2, n], x_to(step))

    def rest_b(half):
        for n in range(4):
            for back in (3 if n % 2 == 0 else 1, 2):
                landed(b_pieces(half, turned(x, -back), turned(y, -STEPS[n])), bx_got.at[half, back, n])

    def pair_up():
        for copy in index_copies:
            copy.wait()
        landed(spots.at[1], c_sem.at[1])
        spot = jnp.where(same, spots[0, 0], spots[1, 0])
        kept_row = jnp.where(spot >= 0, spot // NBL, -2)
        kept_col = jnp.where(spot >= 0, spot % NBL, -2)

        def number_of(index, kept, number):
            slots, groups = index.shape

            def one(g):
                lane = lax.broadcasted_iota(jnp.int32, (slots, groups), 1)
                mine = jnp.sum(jnp.where(lane == g, index, 0), axis=1, keepdims=True)
                return jnp.max(jnp.where(mine == kept, number, -1), axis=0, keepdims=True)

            return one

        u = lax.broadcasted_iota(jnp.int32, (16, BS), 0)
        v = lax.broadcasted_iota(jnp.int32, (8, BS), 0)
        for m in range(4):
            row_of = number_of(rows[m], kept_row, (u >> 1) * 4 + (u & 1))
            col_of = number_of(cols[m], kept_col, (v & 1) * 16 + (v >> 1) * 4)
            for n in range(4):
                a_at, b_at = row_of((y * 2 + core) * 4 + n), col_of((y * 2 + core) * 4 + n)
                code = (a_at + n % 2 * 2) * 64 + b_at + (m // 2 * 32 + m % 2 * 2 + n % 2)
                codes[n * 4 + m : n * 4 + m + 1] = jnp.where((a_at >= 0) & (b_at >= 0), code, NONE)
        copy = pltpu.make_async_copy(codes, jobs, c_sem.at[2])
        copy.start()
        copy.wait()

    def add_products(half, back, first, count, fresh=False, width=32):
        left_ref, right_ref = a_half[half][back], b_half[half]
        k = half * 8 + turned(z, -back)

        def some(n, _):
            for s in range(width):
                slot = first + n * width + s
                one, two = jobs[k, slot], jobs[k + 4, slot]
                left = jnp.concatenate([left_ref[one >> 6], left_ref[two >> 6]], axis=1)
                right = jnp.concatenate([right_ref[one & 63], right_ref[two & 63]], axis=0)
                term = jnp.dot(left, right, preferred_element_type=jnp.float32)
                if fresh:
                    total[slot] = term
                else:
                    total[slot] += term
            return 0

        lax.fori_loop(0, count // width, some, 0)

    hand_out_a(0)
    turn_a(0, 0)
    hand_out_b(0)
    send(c_ref, spots.at[1], c_sem.at[0], c_sem.at[1], twin)
    turn_a(0, 1)
    turn_b(0, 0)
    turn_a(0, 2)
    pass_a(0, 0)
    pass_a(0, 1)
    turn_a(0, 3)
    hand_out_a(1)
    pass_a(0, 2)
    turn_a(0, 4)
    turn_a(0, 5)
    turn_b(0, 1)
    turn_b(0, 2)
    hand_out_b(1)
    turn_b(0, 3)
    pass_a(0, 3)
    pass_b(0, 0)
    pass_b(0, 1)
    pass_a(0, 4)
    pass_a(0, 5)
    pass_b(0, 2)
    pass_b(0, 3)
    pair_up()
    turn_a(1, 0)
    turn_a(1, 1)
    turn_a(1, 2)
    turn_a(1, 3)
    turn_a(1, 4)
    turn_a(1, 5)
    turn_b(1, 0)
    turn_b(1, 1)
    rest_b(0)
    add_products(0, 0, 0, BS, fresh=True)
    turn_b(1, 2)
    turn_b(1, 3)
    rest_a(0, 1)
    add_products(0, 1, 0, BS)
    pass_a(1, 0)
    pass_a(1, 1)
    pass_b(1, 0)
    pass_b(1, 1)
    rest_a(0, 3)
    add_products(0, 3, 0, BS)
    pass_a(1, 2)
    pass_b(1, 2)
    pass_b(1, 3)
    rest_a(0, 2)
    add_products(0, 2, 0, BS)
    pass_a(1, 3)
    rest_b(1)
    add_products(1, 0, 0, BS)
    pass_a(1, 4)
    pass_a(1, 5)
    rest_a(1, 1)
    add_products(1, 1, 0, BS)
    rest_a(1, 3)
    add_products(1, 3, 0, BS)
    rest_a(1, 2)

    def start_of(r):
        return turned(y, r) * 32

    def end_products(r):
        add_products(1, 2, start_of(r) + (1 - core) * 16, 16, width=16)
        for part in range(4):
            span = pl.ds(part * PART, PART)
            send(
                total.at[pl.ds(start_of(r) + (1 - core) * 16 + part * PART, PART)], other.at[r, span],
                twin_sem.at[0, r, part], twin_sem.at[1, r, part], twin,
            )
        add_products(1, 2, start_of(r) + core * 16, 16, width=16)

    def meet(r, part):
        landed(other.at[r, pl.ds(part * PART, PART)], twin_sem.at[1, r, part])

    def arrived(i):
        landed(q_in.at[i], q_recv.at[i])
        landed(s_in.at[i], s_recv.at[i])

    def chip_sum(r, slot):
        return total[start_of(r) + core * 16 + slot] + other[r, slot]

    def value(i, n):
        return q_in[i, n].astype(jnp.float32) * s_in[i, pl.ds(n, 1)]

    def tell(i, step, r, first, plus=None):
        meet(r, first // PART)

        def term(n):
            sums = chip_sum(r, first + n)
            return sums if plus is None else sums + value(plus, n)

        tops = [
            jnp.maximum(jnp.max(jnp.abs(term(n)), axis=0, keepdims=True), TINY) for n in range(PART)
        ]
        for n, top in enumerate(tops):
            s_out[i, n : n + 1] = top * (1 / TOP)
        scales = [TOP / top for top in tops]
        for n, scale in enumerate(scales):
            q_out[i, n] = jnp.round(term(n) * scale).astype(jnp.int32).astype(jnp.int16)
        send(q_out.at[i], q_in.at[i], q_send.at[i], q_recv.at[i], y_to(step))
        send(s_out.at[i], s_in.at[i], s_send.at[i], s_recv.at[i], y_to(step))

    gathered = len(waits)
    end_products(2)
    for part in range(PARTS):
        tell(part, 1, 2, part * PART)
        tell(PARTS + part, -1, 2, 8 + part * PART)
    end_products(1)
    for part in range(PARTS):
        tell(2 * PARTS + part, 1, 1, 8 + part * PART)
    end_products(3)
    for part in range(PARTS // 2):
        tell(3 * PARTS + part, -1, 3, part * PART)
    end_products(0)
    settle(gathered)
    handed = len(waits)
    for part in range(PARTS):
        arrived(PARTS + part)
        tell(5 * PARTS + part, -1, 3, 8 + part * PART, plus=PARTS + part)
        arrived(part)
        tell(4 * PARTS + part, 1, 1, part * PART, plus=part)
    for part in range(PARTS // 2, PARTS):
        tell(3 * PARTS + part, -1, 3, part * PART)

    def finish(part, first, second):
        meet(0, part)
        arrived(first)
        arrived(second)

        def one(n, _):
            slot = part * PART + n
            sums = chip_sum(0, slot) + value(first, n) + value(second, n)
            done[slot] = sums.astype(jnp.bfloat16)
            return 0

        lax.fori_loop(0, PART, one, 0)
        span = pl.ds(part * PART, PART)
        hand_out_here(done.at[span], out_ref.at[span], out_sem.at[0, part], out_sem.at[1, part], owner)

    settle(handed)
    for part in range(PARTS):
        finish(PARTS + part, 2 * PARTS + part, 5 * PARTS + part)
        finish(part, 3 * PARTS + part, 4 * PARTS + part)
    for part in range(2 * PARTS):
        landed(out_ref.at[pl.ds(part * PART, PART)], out_sem.at[1, part])
    settle(len(waits))


def per_device(a_blocks, a_rows, b_blocks, b_cols, c_pos):
    rows, cols = a_rows.transpose(1, 2, 3, 0), b_cols.transpose(1, 2, 3, 0)
    dma = pltpu.SemaphoreType.DMA
    vmem = pl.BlockSpec(memory_space=pltpu.VMEM)
    bf16, f32, i16, i32 = jnp.bfloat16, jnp.float32, jnp.int16, jnp.int32
    out = pl.pallas_call(
        kernel,
        out_shape=jax.ShapeDtypeStruct((16, BS, BS), bf16),
        in_specs=[pl.BlockSpec(memory_space=pltpu.HBM)] * 5,
        out_specs=vmem,
        scratch_shapes=[
            *[pltpu.VMEM((ZERO + 1, BS, BS), bf16)] * 8,
            *[pltpu.VMEM((64, BS, BS), bf16)] * 2,
            pltpu.VMEM((2,) + c_pos.shape, i32),
            pltpu.VMEM((4, 16, 32), i32),
            pltpu.VMEM((4, 8, 32), i32),
            pltpu.VMEM((16, BS), i32),
            pltpu.SMEM((16, BS), i32),
            pltpu.VMEM((BS, BS, BS), f32),
            pltpu.VMEM((4, 16, BS, BS), f32),
            pltpu.VMEM((16, BS, BS), bf16),
            pltpu.VMEM((6 * PARTS, PART, BS, BS), i16),
            pltpu.VMEM((6 * PARTS, PART, BS), f32),
            pltpu.VMEM((6 * PARTS, PART, BS, BS), i16),
            pltpu.VMEM((6 * PARTS, PART, BS), f32),
            dma((2, 8)), dma((2, 8)), dma((2, 4, 6)), dma((2, 4, 6)),
            dma((2, 8)), dma((2, 8)), dma((2, 4, 4)), dma((2, 4, 4)), dma((5,)),
            dma((2, 4, 2 * PARTS)), *[dma((6 * PARTS,))] * 4, dma((2, 2 * PARTS)),
        ],
        compiler_params=pltpu.CompilerParams(
            collective_id=0, has_side_effects=True, vmem_limit_bytes=44 * 2**20
        ),
        name="block_product",
    )(*(pltpu.with_memory_space_constraint(x, pltpu.HBM) for x in (a_blocks.reshape(64, BS, BS), b_blocks.reshape(32, BS, BS), c_pos, rows, cols)))
    return out[None, None]


def solution(mesh):
    placed = (
        P(None, "col", "row", "depth", None, None),
        P(),
        P(None, "row", "col", "depth", None, None),
        P(),
        P("row", "col", None),
    )
    return jax.shard_map(
        per_device,
        mesh=mesh,
        in_specs=placed,
        out_specs=P("row", "col", "depth", None, None),
        check_vma=False,
    )
```

```python
import jax
import jax.numpy as jnp
from jax import lax
from jax.experimental import pallas as pl
from jax.experimental.pallas import tpu as pltpu
from jax.sharding import PartitionSpec as P

MESH = pl.DeviceIdType.MESH
BS = 128
NBL = 16
ANY = pl.BlockSpec(memory_space=pl.ANY)


def place():
    row, z, depth = lax.axis_index("row"), lax.axis_index("col"), lax.axis_index("depth")
    return row // 2, depth % 2, row % 2, depth // 2, z


def device(x_hi, x_lo, core, y, z):
    return (x_hi * 2 + core, z, y * 2 + x_lo)


def remote(src, dst, send, recv, to):
    return pltpu.make_async_remote_copy(
        src_ref=src, dst_ref=dst, send_sem=send, recv_sem=recv, device_id=to, device_id_type=MESH
    )


STEPS = (0, 1, 3, 2)
UNITS = ((0, 0), (0, 1), (1, None), (2, None), (3, 0), (3, 1))
TOP = 32767.0
TINY = 2e-34
PART = 4
PARTS = 8 // PART
ZERO = 32
NONE = ZERO * 64


def kernel(
    a_ref, b_ref, c_ref, rows_ref, cols_ref, out_ref,
    a00, a01, a02, a03, a10, a11, a12, a13, b0, b1, spots, rows, cols, codes, jobs, total, other, done, q_out, s_out, q_in, s_in,
    az_out, az_recv, az_ring, az_got, bx_out, bx_recv, bx_ring, bx_got, c_sem,
    twin_sem, q_send, q_recv, s_send, s_recv, out_sem,
):
    x_hi, x_lo, core, y, z = place()
    x = x_hi * 2 + x_lo
    same = x_lo == core
    apart = jnp.where(same, 0, 1)
    a_half, b_half = ((a00, a01, a02, a03), (a10, a11, a12, a13)), (b0, b1)

    def turned(at, step):
        return lax.rem(at + step + 8, 4)

    def differ(at, flag):
        return at if flag == 0 else 1 - at

    def z_to(step):
        return device(x_hi, x_lo, core, y, turned(z, step))

    def x_to(step):
        to = turned(x, step)
        return device(to // 2, lax.rem(to, 2), core, y, z)

    def y_to(step):
        return device(x_hi, x_lo, core, turned(y, step), z)

    twin = device(x_hi, x_lo, 1 - core, y, z)
    owner = device(x_hi, core, x_lo, y, z)

    barrier = pltpu.get_barrier_semaphore()

    def greet(to):
        pl.semaphore_signal(barrier, inc=1, device_id=to, device_id_type=MESH)

    for dy in STEPS:
        for flag in range(2):
            if (dy, flag) == (0, 0):

                @pl.when(jnp.logical_not(same))
                def _():
                    greet(twin)

            else:
                greet(device(x_hi, differ(x_lo, flag), x_lo, turned(y, -dy), z))
                greet(device(x_hi, x_lo, differ(core, flag), turned(y, -dy), z))
    for step in (1, -1):
        greet(z_to(step))
        greet(x_to(step))
    index_copies = [
        pltpu.make_async_copy(c_ref, spots.at[0], c_sem.at[2]),
        pltpu.make_async_copy(rows_ref.at[:, x], rows, c_sem.at[3]),
        pltpu.make_async_copy(cols_ref.at[:, z], cols, c_sem.at[4]),
    ]
    for copy in index_copies:
        copy.start()
    for half in a_half:
        for ref in half:
            ref[ZERO] = jnp.zeros((BS, BS), jnp.bfloat16)
    pl.semaphore_wait(barrier, 18 + apart)

    waits = []

    def send(src, dst, sent, recv, to):
        copy = remote(src, dst, sent, recv, to)
        copy.start()
        waits.append(copy.wait_send)

    def settle(count):
        for _ in range(count):
            waits.pop(0)()

    def landed(piece, recv):
        remote(piece, piece, recv, recv, twin).wait_recv()

    def a_piece(half, back, at_y, at_lo):
        return a_half[half][back].at[pl.ds(at_y * 8 + at_lo * 4, 4)]

    def a_pieces(half, back, at_y):
        return a_half[half][back].at[pl.ds(at_y * 8, 8)]

    def b_piece(half, at_x, at_y, at_core):
        return b_half[half].at[pl.ds(at_x * 16 + at_y * 4 + at_core * 2, 2)]

    def b_pieces(half, at_x, at_y):
        return b_half[half].at[pl.ds(at_x * 16 + at_y * 4, 4)]

    def hand_out_a(half):
        for n, dy in enumerate(STEPS):
            for flag in range(2):
                to_y, to_core = turned(y, dy), differ(core, flag)
                group = (to_y * 2 + to_core) * 4 + half * 2
                src, dst = a_ref.at[pl.ds(group * 2, 4)], a_piece(half, 0, y, x_lo)
                sent, recv = az_out.at[half, n * 2 + flag], az_recv.at[half, n * 2 + apart]
                to = device(x_hi, core, to_core, to_y, z)
                if (dy, flag) == (0, 0):
                    hand_out_here(src, dst, sent, recv, to)
                else:
                    send(src, dst, sent, recv, to)

    def hand_out_b(half):
        for n, dy in enumerate(STEPS):
            for flag in range(2):
                to_y, to_core = turned(y, dy), differ(core, flag)
                group = (to_y * 2 + to_core) * 4 + half * 2
                src, dst = b_ref.at[pl.ds(group, 2)], b_piece(half, x, y, core)
                sent, recv = bx_out.at[half, n * 2 + flag], bx_recv.at[half, n * 2 + flag]
                if (dy, flag) == (0, 0):
                    pltpu.make_async_copy(src, dst, recv).start()
                else:
                    send(src, dst, sent, recv, device(x_hi, x_lo, to_core, to_y, z))

    def hand_out_here(src, dst, sent, recv, to):
        copy = remote(src, dst, sent, recv, to)
        stay = pltpu.make_async_copy(src, dst, recv)
        pl.when(same)(lambda: stay.start())
        pl.when(jnp.logical_not(same))(lambda: copy.start())
        waits.append(lambda: pl.when(jnp.logical_not(same))(lambda: copy.wait_send()))

    def a_unit(half, back, i):
        n, flag = UNITS[i]
        at = turned(y, -STEPS[n])
        return a_pieces(half, back, at) if flag is None else a_piece(half, back, at, differ(x_lo, flag))

    def turn_a(half, i):
        n, flag = UNITS[i]
        for one in range(2) if flag is None else (flag,):
            piece = a_piece(half, 0, turned(y, -STEPS[n]), differ(x_lo, one))
            landed(piece, az_recv.at[half, n * 2 + one])
        for back, step in ((1, 1), (3, -1)):
            send(
                a_unit(half, 0, i), a_unit(half, back, i), az_ring.at[half, back, i], az_got.at[half, back, i],
                z_to(step),
            )

    def pass_a(half, i):
        back, step = (1, 1) if i % 2 == 0 else (3, -1)
        landed(a_unit(half, back, i), az_got.at[half, back, i])
        send(
            a_unit(half, back, i), a_unit(half, 2, i), az_ring.at[half, 2, i], az_got.at[half, 2, i], z_to(step)
        )

    def rest_a(half, back):
        for i in range(len(UNITS)):
            if back == 2 or back != (1 if i % 2 == 0 else 3):
                landed(a_unit(half, back, i), az_got.at[half, back, i])

    def turn_b(half, n):
        at = turned(y, -STEPS[n])
        for flag in range(2):
            landed(b_piece(half, x, at, differ(core, flag)), bx_recv.at[half, n * 2 + flag])
        here = b_pieces(half, x, at)
        for back, step in ((1, 1), (3, -1)):
            send(here, here, bx_ring.at[half, back, n], bx_got.at[half, back, n], x_to(step))

    def pass_b(half, n):
        back, step = (1, 1) if n % 2 == 0 else (3, -1)
        there = b_pieces(half, turned(x, -back), turned(y, -STEPS[n]))
        landed(there, bx_got.at[half, back, n])
        send(there, there, bx_ring.at[half, 2, n], bx_got.at[half, 2, n], x_to(step))

    def rest_b(half):
        for n in range(4):
            for back in (3 if n % 2 == 0 else 1, 2):
                landed(b_pieces(half, turned(x, -back), turned(y, -STEPS[n])), bx_got.at[half, back, n])

    def pair_up():
        for copy in index_copies:
            copy.wait()
        landed(spots.at[1], c_sem.at[1])
        spot = jnp.where(same, spots[0, 0], spots[1, 0])
        kept_row = jnp.where(spot >= 0, spot // NBL, -2)
        kept_col = jnp.where(spot >= 0, spot % NBL, -2)

        def number_of(index, kept, number):
            slots, groups = index.shape

            def one(g):
                lane = lax.broadcasted_iota(jnp.int32, (slots, groups), 1)
                mine = jnp.sum(jnp.where(lane == g, index, 0), axis=1, keepdims=True)
                return jnp.max(jnp.where(mine == kept, number, -1), axis=0, keepdims=True)

            return one

        u = lax.broadcasted_iota(jnp.int32, (16, BS), 0)
        v = lax.broadcasted_iota(jnp.int32, (8, BS), 0)
        for m in range(4):
            row_of = number_of(rows[m], kept_row, (u >> 1) * 4 + (u & 1))
            col_of = number_of(cols[m], kept_col, (v & 1) * 16 + (v >> 1) * 4)
            for n in range(4):
                a_at, b_at = row_of((y * 2 + core) * 4 + n), col_of((y * 2 + core) * 4 + n)
                code = (a_at + n % 2 * 2) * 64 + b_at + (m // 2 * 32 + m % 2 * 2 + n % 2)
                codes[n * 4 + m : n * 4 + m + 1] = jnp.where((a_at >= 0) & (b_at >= 0), code, NONE)
        copy = pltpu.make_async_copy(codes, jobs, c_sem.at[2])
        copy.start()
        copy.wait()

    def add_products(half, back, first, count, fresh=False, width=32):
        left_ref, right_ref = a_half[half][back], b_half[half]
        k = half * 8 + turned(z, -back)

        def some(n, _):
            for s in range(width):
                slot = first + n * width + s
                one, two = jobs[k, slot], jobs[k + 4, slot]
                left = jnp.concatenate([left_ref[one >> 6], left_ref[two >> 6]], axis=1)
                right = jnp.concatenate([right_ref[one & 63], right_ref[two & 63]], axis=0)
                term = jnp.dot(left, right, preferred_element_type=jnp.float32)
                if fresh:
                    total[slot] = term
                else:
                    total[slot] += term
            return 0

        lax.fori_loop(0, count // width, some, 0)

    hand_out_a(0)
    turn_a(0, 0)
    send(c_ref, spots.at[1], c_sem.at[0], c_sem.at[1], twin)
    turn_a(0, 1)
    hand_out_b(0)
    turn_b(0, 0)
    turn_a(0, 2)
    pass_a(0, 0)
    pass_a(0, 1)
    turn_a(0, 3)
    pass_a(0, 2)
    turn_a(0, 4)
    turn_a(0, 5)
    turn_b(0, 1)
    turn_b(0, 2)
    hand_out_a(1)
    hand_out_b(1)
    turn_b(0, 3)
    pass_a(0, 3)
    pass_b(0, 0)
    pass_b(0, 1)
    pass_a(0, 4)
    pass_a(0, 5)
    pass_b(0, 2)
    pass_b(0, 3)
    pair_up()
    turn_a(1, 0)
    turn_a(1, 1)
    turn_a(1, 2)
    turn_a(1, 3)
    turn_a(1, 4)
    turn_a(1, 5)
    turn_b(1, 0)
    turn_b(1, 1)
    rest_b(0)
    add_products(0, 0, 0, BS, fresh=True)
    turn_b(1, 2)
    turn_b(1, 3)
    rest_a(0, 1)
    add_products(0, 1, 0, BS)
    pass_a(1, 0)
    pass_a(1, 1)
    pass_b(1, 0)
    pass_b(1, 1)
    rest_a(0, 3)
    add_products(0, 3, 0, BS)
    pass_a(1, 2)
    pass_b(1, 2)
    pass_b(1, 3)
    rest_a(0, 2)
    add_products(0, 2, 0, BS)
    pass_a(1, 3)
    rest_b(1)
    add_products(1, 0, 0, BS)
    pass_a(1, 4)
    pass_a(1, 5)
    rest_a(1, 1)
    add_products(1, 1, 0, BS)
    rest_a(1, 3)
    add_products(1, 3, 0, BS)
    rest_a(1, 2)

    def start_of(r):
        return turned(y, r) * 32

    def end_products(r):
        add_products(1, 2, start_of(r) + (1 - core) * 16, 16, width=16)
        for part in range(4):
            span = pl.ds(part * PART, PART)
            send(
                total.at[pl.ds(start_of(r) + (1 - core) * 16 + part * PART, PART)], other.at[r, span],
                twin_sem.at[0, r, part], twin_sem.at[1, r, part], twin,
            )
        add_products(1, 2, start_of(r) + core * 16, 16, width=16)

    def meet(r, part):
        landed(other.at[r, pl.ds(part * PART, PART)], twin_sem.at[1, r, part])

    def arrived(i):
        landed(q_in.at[i], q_recv.at[i])
        landed(s_in.at[i], s_recv.at[i])

    def chip_sum(r, slot):
        return total[start_of(r) + core * 16 + slot] + other[r, slot]

    def value(i, n):
        return q_in[i, n].astype(jnp.float32) * s_in[i, pl.ds(n, 1)]

    def tell(i, step, r, first, plus=None):
        meet(r, first // PART)

        def term(n):
            sums = chip_sum(r, first + n)
            return sums if plus is None else sums + value(plus, n)

        tops = [
            jnp.maximum(jnp.max(jnp.abs(term(n)), axis=0, keepdims=True), TINY) for n in range(PART)
        ]
        for n, top in enumerate(tops):
            s_out[i, n : n + 1] = top * (1 / TOP)
        scales = [TOP / top for top in tops]
        for n, scale in enumerate(scales):
            q_out[i, n] = jnp.round(term(n) * scale).astype(jnp.int32).astype(jnp.int16)
        send(q_out.at[i], q_in.at[i], q_send.at[i], q_recv.at[i], y_to(step))
        send(s_out.at[i], s_in.at[i], s_send.at[i], s_recv.at[i], y_to(step))

    gathered = len(waits)
    end_products(2)
    for part in range(PARTS):
        tell(part, 1, 2, part * PART)
        tell(PARTS + part, -1, 2, 8 + part * PART)
    end_products(1)
    for part in range(PARTS):
        tell(2 * PARTS + part, 1, 1, 8 + part * PART)
    end_products(3)
    for part in range(PARTS // 2):
        tell(3 * PARTS + part, -1, 3, part * PART)
    end_products(0)
    settle(gathered)
    handed = len(waits)
    for part in range(PARTS):
        arrived(PARTS + part)
        tell(5 * PARTS + part, -1, 3, 8 + part * PART, plus=PARTS + part)
        arrived(part)
        tell(4 * PARTS + part, 1, 1, part * PART, plus=part)
    for part in range(PARTS // 2, PARTS):
        tell(3 * PARTS + part, -1, 3, part * PART)

    def finish(part, first, second):
        meet(0, part)
        arrived(first)
        arrived(second)

        def one(n, _):
            slot = part * PART + n
            sums = chip_sum(0, slot) + value(first, n) + value(second, n)
            done[slot] = sums.astype(jnp.bfloat16)
            return 0

        lax.fori_loop(0, PART, one, 0)
        span = pl.ds(part * PART, PART)
        hand_out_here(done.at[span], out_ref.at[span], out_sem.at[0, part], out_sem.at[1, part], owner)

    settle(handed)
    for part in range(PARTS):
        finish(PARTS + part, 2 * PARTS + part, 5 * PARTS + part)
        finish(part, 3 * PARTS + part, 4 * PARTS + part)
    for part in range(2 * PARTS):
        landed(out_ref.at[pl.ds(part * PART, PART)], out_sem.at[1, part])
    settle(len(waits))


def per_device(a_blocks, a_rows, b_blocks, b_cols, c_pos):
    rows, cols = a_rows.transpose(1, 2, 3, 0), b_cols.transpose(1, 2, 3, 0)
    dma = pltpu.SemaphoreType.DMA
    vmem = pl.BlockSpec(memory_space=pltpu.VMEM)
    bf16, f32, i16, i32 = jnp.bfloat16, jnp.float32, jnp.int16, jnp.int32
    out = pl.pallas_call(
        kernel,
        out_shape=jax.ShapeDtypeStruct((16, BS, BS), bf16),
        in_specs=[pl.BlockSpec(memory_space=pltpu.HBM)] * 5,
        out_specs=vmem,
        scratch_shapes=[
            *[pltpu.VMEM((ZERO + 1, BS, BS), bf16)] * 8,
            *[pltpu.VMEM((64, BS, BS), bf16)] * 2,
            pltpu.VMEM((2,) + c_pos.shape, i32),
            pltpu.VMEM((4, 16, 32), i32),
            pltpu.VMEM((4, 8, 32), i32),
            pltpu.VMEM((16, BS), i32),
            pltpu.SMEM((16, BS), i32),
            pltpu.VMEM((BS, BS, BS), f32),
            pltpu.VMEM((4, 16, BS, BS), f32),
            pltpu.VMEM((16, BS, BS), bf16),
            pltpu.VMEM((6 * PARTS, PART, BS, BS), i16),
            pltpu.VMEM((6 * PARTS, PART, BS), f32),
            pltpu.VMEM((6 * PARTS, PART, BS, BS), i16),
            pltpu.VMEM((6 * PARTS, PART, BS), f32),
            dma((2, 8)), dma((2, 8)), dma((2, 4, 6)), dma((2, 4, 6)),
            dma((2, 8)), dma((2, 8)), dma((2, 4, 4)), dma((2, 4, 4)), dma((5,)),
            dma((2, 4, 2 * PARTS)), *[dma((6 * PARTS,))] * 4, dma((2, 2 * PARTS)),
        ],
        compiler_params=pltpu.CompilerParams(
            collective_id=0, has_side_effects=True, vmem_limit_bytes=44 * 2**20
        ),
        name="block_product",
    )(*(pltpu.with_memory_space_constraint(x, pltpu.HBM) for x in (a_blocks.reshape(64, BS, BS), b_blocks.reshape(32, BS, BS), c_pos, rows, cols)))
    return out[None, None]


def solution(mesh):
    placed = (
        P(None, "col", "row", "depth", None, None),
        P(),
        P(None, "row", "col", "depth", None, None),
        P(),
        P("row", "col", None),
    )
    return jax.shard_map(
        per_device,
        mesh=mesh,
        in_specs=placed,
        out_specs=P("row", "col", "depth", None, None),
        check_vma=False,
    )
```
